128 devices in a mesh: prow: 8 (over x, core), pcol: 16 (over z, y).
Axes of the slice: x: 4, y: 4, z: 4, core: 2. Of those that a mesh axis runs over, the one named last changes fastest.
Arguments:
- matrix: float32 [8, 16, 768, 384], P('prow', 'pcol'), may hold values from -6 to 6
- pivots: int32 [3, 384], replicated, may hold values from 0 to 6143, as said below
- lower_inv: float32 [3, 384, 384], replicated, may hold values from -0.3125 to 0.3125
- upper_inv: float32 [3, 384, 384], replicated, may hold values from -0.015625 to 0.015625
Outputs:
- factored: float32 [8, 16, 768, 384], P('prow', 'pcol')
The draws below stay inside these ranges and needn't reach their ends.
Inputs may be any that keep to these rules, and one draw needn't show every extreme that they name: Within one step s the indices pivots[s, i] are distinct, and each equals s * 384 + i or lies between (s + 1) * 384 and 6143.
All inputs are finite; a program needn't handle non-finite values.
Results may differ from the reference program's by a relative error of at most 0.0002.
Values sent between devices are 32-bit elements; how exact they have to be, the bound alone decides.
No kernel may reach another device: no remote copies, remote signals or barrier semaphores. Data moves between devices by JAX's collectives and lax.ppermute only.
A program may use at most 64 MiB of HBM per device.

```python
import jax
import jax.numpy as jnp
from jax import lax

NB = 384
ROWB = 2
STEPS = 3
ORDER = 6144
COLB = 1
N_PROW = 8
N_PCOL = 16


def draw_pivots(key, part):
    offsets = jnp.arange(NB, dtype=jnp.int32)
    listed = []
    for section in range(STEPS):
        section_key = jax.random.fold_in(key, 7919 + section)
        first = section * NB
        finish = first + NB
        shuffled = jax.random.permutation(jax.random.fold_in(section_key, 1), ORDER - finish)[:NB].astype(jnp.int32) + finish
        staying = jax.random.randint(jax.random.fold_in(section_key, 2), (NB,), 0, 4, dtype=jnp.int32) == 0
        listed.append(jnp.where(staying, first + offsets, shuffled).astype(jnp.int32))
    return jnp.stack(listed).astype(jnp.int32)


def steps_of(rng, shape, shards, low, high):
    gain = 1.0
    for axis_at, parts in shards:
        steps = jax.random.uniform(jax.random.fold_in(jax.random.fold_in(rng, 6), axis_at), (parts,), jnp.float32, low / len(shards), high / len(shards))
        gain = gain * jnp.repeat(jnp.exp(steps), shape[axis_at] // parts).reshape((-1,) + (1,) * (len(shape) - 1 - axis_at))
    return gain


def centred(key, extent, scale, bound, cuts=(), kind=jnp.bfloat16):
    drawn = jax.random.normal(key, extent, jnp.float32) * scale
    if len(cuts) > 0:
        drawn = steps_of(key, extent, cuts, -0.22, 0.18) * drawn
    return jnp.clip(drawn, min=-bound, max=bound).astype(kind)


def setup_inputs(seed: int = 0) -> dict:
    arg_keys = jax.random.split(jax.random.key(seed), 5)
    matrix = centred(arg_keys[0], (N_PROW, N_PCOL, ROWB * NB, COLB * NB), 1.0, 6.0, ((0, 8), (1, 16)), jnp.float32)
    pivots = draw_pivots(jax.random.fold_in(arg_keys[4], 71), 0)
    lower_inv = centred(arg_keys[2], (STEPS, NB, NB), NB ** -0.5, 0.3125, (), jnp.float32)
    upper_inv = centred(arg_keys[3], (STEPS, NB, NB), (NB * NB) ** -0.5, 0.015625, (), jnp.float32)
    return dict(matrix=matrix, pivots=pivots, lower_inv=lower_inv, upper_inv=upper_inv)


def compose(pivot_list, first):
    identity = jnp.arange(ORDER, dtype=jnp.int32)

    def exchange_pair(position, permutation):
        target = (first + position).astype(jnp.int32)
        source = pivot_list[position]
        held_here = permutation[target]
        held_there = permutation[source]
        return permutation.at[target].set(held_there).at[source].set(held_here)

    return lax.fori_loop(0, NB, exchange_pair, identity)


def reference(matrix, pivots, lower_inv, upper_inv):
    precise = lax.Precision.HIGHEST
    whole = matrix.reshape(N_PROW, N_PCOL, ROWB, NB, COLB, NB).transpose(2, 0, 3, 4, 1, 5).reshape(ORDER, ORDER)
    offsets = jnp.arange(NB, dtype=jnp.int32)
    for section in range(STEPS):
        start = section * NB
        finish = start + NB
        pivot_list = pivots[section]
        permutation = compose(pivot_list, start)
        targets = jnp.concatenate([(start + offsets).astype(jnp.int32), pivot_list.astype(jnp.int32)])
        sources = permutation[targets]
        whole = whole.at[targets].set(whole[sources])
        lower_unit = jnp.eye(NB, dtype=jnp.float32) + jnp.tril(lower_inv[section], -1)
        upper_tri = jnp.triu(upper_inv[section])
        upper_rows = jnp.dot(lower_unit, whole[start:finish, finish:], precision=precise, preferred_element_type=jnp.float32)
        lower_panel = jnp.dot(whole[finish:, start:finish], upper_tri, precision=precise, preferred_element_type=jnp.float32)
        whole = whole.at[start:finish, finish:].set(upper_rows)
        whole = whole.at[finish:, start:finish].set(lower_panel)
        update = jnp.dot(lower_panel, upper_rows, precision=precise, preferred_element_type=jnp.float32)
        whole = whole.at[finish:, finish:].set(whole[finish:, finish:] - update)
    return whole.reshape(ROWB, N_PROW, NB, COLB, N_PCOL, NB).transpose(1, 4, 0, 2, 3, 5).reshape(N_PROW, N_PCOL, ROWB * NB, COLB * NB)
```

```python
import jax
import jax.numpy as jnp
from jax import lax
from jax.sharding import PartitionSpec as P

HIGH = lax.Precision.HIGH
EXACT = lax.Precision.HIGHEST
W = 384
STEPS = 3
NX, NZ, NY = 4, 4, 4
PROWS, PCOLS = 8, 16
TOP = STEPS * W
SUB = W // PROWS
COLS = W // PCOLS


def mm(a, b):
    return jnp.dot(a, b, precision=HIGH, preferred_element_type=jnp.float32)


def x_shift(v, k):
    return lax.ppermute(v, "prow", [(p, (p + 2 * k) % PROWS) for p in range(PROWS)])


def x_shift_top(v, k):
    return lax.ppermute(v, "prow", [(p, (p + 2 * k) % PROWS) for p in range(STEPS)])


def sibling(v):
    return lax.ppermute(v, "prow", [(p, p ^ 1) for p in range(PROWS)])


def y_shift(v, k):
    return lax.ppermute(
        v, "pcol", [(z * NY + y, z * NY + (y + k) % NY) for z in range(NZ) for y in range(NY)]
    )


def from_z0(v, k):
    return lax.ppermute(v, "pcol", [(y, k * NY + y) for y in range(STEPS)])


def swapped(v, pivot_list, section):
    here = section * W + jnp.arange(W, dtype=jnp.int32)
    at = v[:, None]
    moves = jnp.where(at == pivot_list[None, :], here[None, :] - at, 0)
    moves = moves + jnp.where(at == here[None, :], pivot_list[None, :] - at, 0)
    return v + moves.sum(axis=1)


def origin(v, pivots):
    for section in reversed(range(STEPS)):
        v = swapped(v, pivots[section], section)
    return v


def placed(parts, places, axis):
    shape = parts[0].shape
    whole = jnp.zeros(shape[:axis] + (len(parts),) + shape[axis:], parts[0].dtype)
    for part, place in zip(parts, places):
        whole = lax.dynamic_update_slice_in_dim(whole, jnp.expand_dims(part, axis), place, axis=axis)
    return whole


def top_rows_everywhere(block, x, core):
    got = [x_shift_top(block, k) for k in (1, 2, 3)]
    mine = jnp.where(x == 0, block, 0)
    first = mine + jnp.where(x == 1, got[0], 0) + jnp.where(x == 2, got[1], 0) + jnp.where(x == 3, got[2], 0)
    mine = jnp.where((x == 1) & (core == 0), block, 0)
    second = mine + jnp.where(x == 2, got[0], 0) + jnp.where(x == 3, got[1], 0) + jnp.where(x == 0, got[2], 0)
    pair = jnp.stack([first, second])
    other = sibling(pair)
    low = jnp.where(core == 0, pair, other)
    high = jnp.where(core == 0, other, pair)
    return low[0], high[0], low[1]


def on_device(matrix, pivots, lower_inv, upper_inv):
    p = lax.axis_index("prow")
    q = lax.axis_index("pcol")
    x, core = p // 2, p % 2
    z, y = q // NY, q % NY
    tile = matrix[0, 0]
    rows = tile.shape[0]

    slots = jnp.arange(PROWS, dtype=jnp.int32)
    piece = ((x + slots % NX) % NX) * 2 + (core ^ (slots // NX))
    wanted = (
        piece[:, None, None] * SUB
        + (jnp.arange(STEPS, dtype=jnp.int32) * W)[None, :, None]
        + jnp.arange(SUB, dtype=jnp.int32)[None, None, :]
    ).reshape(-1)
    source = origin(wanted, pivots)
    block = source // W
    owned = block % PROWS == p
    local = jnp.where(owned, block // PROWS * W + source % W, 0)
    sent = jnp.where(owned[:, None], tile[local], 0.0).reshape(2, NX, STEPS * SUB, W)
    summed = sent[0] + sibling(sent[1])
    chunk = summed[0]
    for k in (1, 2, 3):
        chunk = chunk + x_shift(summed[k], k)

    parts = chunk.reshape(STEPS, SUB, W)
    twice = jnp.concatenate([parts, parts])
    off = lax.dynamic_slice_in_dim(twice, (y + 1) % STEPS, 2, axis=0)
    spread = jnp.where(z == 0, off, 0.0)
    for k in (1, 2, 3):
        spread = spread + from_z0(off, k)
    line = [spread] + [y_shift(spread, k) for k in (1, 2, 3)]
    line = placed(line, [(y - k) % NY for k in range(NY)], 0)[:STEPS]
    ring = [line] + [x_shift(line, k) for k in (1, 2, 3)]
    ring = ring + [sibling(v) for v in ring]
    held = [(x - k) % NX * 2 + (core ^ side) for side in (0, 1) for k in range(NX)]
    corner = placed(ring, held, 2).reshape(STEPS, 2, W, W)
    a10, a20 = corner[0, 0], corner[0, 1]
    a21, a01 = corner[1, 0], corner[1, 1]
    a02, a12 = corner[2, 0], corner[2, 1]

    near = [chunk] + [x_shift(chunk, k) for k in (1, 2, 3)]
    near = near + [sibling(v) for v in near]
    own = placed([v.reshape(STEPS, SUB, W) for v in near], held, 1).reshape(STEPS, W, W)
    z0, z1, z2 = own[0], own[1], own[2]

    flat = tile.T
    part = jnp.where(z == 0, flat[: W // NZ], 0.0)
    for k in (1, 2, 3):
        part = part + from_z0(flat[k * (W // NZ) : (k + 1) * (W // NZ)], k)
    part = part.reshape(NY, COLS, rows)
    cut = [lax.dynamic_index_in_dim(part, (y + k) % NY, keepdims=False) for k in range(NY)]
    strips = cut[:1] + [y_shift(cut[k], k) for k in (1, 2, 3)]
    strips = placed(strips, [(y - k) % NY for k in range(NY)], 0)[:STEPS].reshape(STEPS * COLS, rows)
    tops = top_rows_everywhere(strips[:, :W], x, core)
    ids = jnp.arange(rows, dtype=jnp.int32)
    global_rows = (ids // W * PROWS + p) * W + ids % W
    came = origin(global_rows, pivots)
    is_bottom = global_rows >= TOP
    moved = is_bottom & (came < TOP)
    pick = jnp.where(moved, rows + came, ids)
    table = jnp.concatenate([strips, *tops], axis=1)
    chooser = (jnp.arange(rows + TOP, dtype=jnp.int32)[:, None] == pick[None, :]).astype(jnp.float32)
    strips = jnp.dot(table, chooser, precision=EXACT, preferred_element_type=jnp.float32)
    panel = lax.all_gather(strips, "pcol")
    panel = panel.reshape(PCOLS, STEPS, COLS, rows).transpose(1, 0, 2, 3).reshape(TOP, rows)

    own_tops = jnp.concatenate(top_rows_everywhere(tile[:W], x, core))
    here = jnp.where(moved[:, None], own_tops[jnp.where(moved, came, 0)], tile)

    eye = jnp.eye(W, dtype=jnp.float32)
    low = eye + jnp.tril(lower_inv, -1)
    up = jnp.triu(upper_inv)
    l10, l20 = mm(a10, up[0]), mm(a20, up[0])
    u01, u02 = mm(low[0], a01), mm(low[0], a02)
    u12 = mm(low[1], a12 - mm(l10, u02))
    l21 = mm(a21 - mm(l20, u01), up[1])
    u0 = mm(low[0], z0)
    x1 = z1 - mm(l10, u0)
    u1 = mm(low[1], x1)
    x2 = z2 - mm(l20, u0) - mm(l21, u1)
    u2 = mm(low[2], x2)

    def basis(t, value):
        return jnp.where(q >= STEPS, value, jnp.where(q == t, -eye, 0.0))

    g2 = mm(up[2], basis(2, u2))
    g1 = mm(up[1], basis(1, u1) - mm(u12, g2))
    g0 = mm(up[0], basis(0, u0) - mm(u01, g1) - mm(u02, g2))
    change = lax.dot_general(
        panel,
        jnp.concatenate([g0, g1, g2]),
        (((0,), (0,)), ((), ())),
        precision=HIGH,
        preferred_element_type=jnp.float32,
    )
    result = jnp.where(q >= STEPS, here, 0.0) - change
    head0 = jnp.where(q == 0, z0, u0)
    head1 = jnp.where(q == 0, l10, jnp.where(q == 1, x1, u1))
    head2 = jnp.where(q == 0, l20, jnp.where(q == 1, l21, jnp.where(q == 2, x2, u2)))
    head = jnp.where(p == 0, head0, jnp.where(p == 1, head1, head2))
    first = jnp.where(p < STEPS, head, result[:W])
    return jnp.concatenate([first, result[W:]])[None, None]


def solution(mesh):
    return jax.shard_map(
        on_device,
        mesh=mesh,
        in_specs=(P("prow", "pcol", None, None), P(), P(), P()),
        out_specs=P("prow", "pcol", None, None),
        check_vma=False,
    )
```

```python
import jax
import jax.numpy as jnp
from jax import lax
from jax.experimental import pallas as pl
from jax.experimental.pallas import tpu as pltpu
from jax.sharding import PartitionSpec as P

HIGH = lax.Precision.HIGH
EXACT = lax.Precision.HIGHEST
W = 384
STEPS = 3
NX, NZ, NY = 4, 4, 4
PROWS, PCOLS = 8, 16
TOP = STEPS * W
SUB = W // PROWS
COLS = W // PCOLS


def x_shift(v, k):
    return lax.ppermute(v, "prow", [(p, (p + 2 * k) % PROWS) for p in range(PROWS)])


def x_shift_top(v, k):
    return lax.ppermute(v, "prow", [(p, (p + 2 * k) % PROWS) for p in range(STEPS)])


def sibling(v):
    return lax.ppermute(v, "prow", [(p, p ^ 1) for p in range(PROWS)])


def y_shift(v, k):
    return lax.ppermute(
        v, "pcol", [(z * NY + y, z * NY + (y + k) % NY) for z in range(NZ) for y in range(NY)]
    )


def from_z0(v, k):
    return lax.ppermute(v, "pcol", [(y, k * NY + y) for y in range(STEPS)])


def swapped(v, pivot_list, section):
    here = section * W + jnp.arange(W, dtype=jnp.int32)
    at = v[:, None]
    moves = jnp.where(at == pivot_list[None, :], here[None, :] - at, 0)
    moves = moves + jnp.where(at == here[None, :], pivot_list[None, :] - at, 0)
    return v + moves.sum(axis=1)


def origin(v, pivots):
    for section in reversed(range(STEPS)):
        v = swapped(v, pivots[section], section)
    return v


def placed(parts, places, axis):
    shape = parts[0].shape
    whole = jnp.zeros(shape[:axis] + (len(parts),) + shape[axis:], parts[0].dtype)
    for part, place in zip(parts, places):
        whole = lax.dynamic_update_slice_in_dim(whole, jnp.expand_dims(part, axis), place, axis=axis)
    return whole


def top_rows_everywhere(block, x, core):
    got = [x_shift_top(block, k) for k in (1, 2, 3)]
    mine = jnp.where(x == 0, block, 0)
    first = mine + jnp.where(x == 1, got[0], 0) + jnp.where(x == 2, got[1], 0) + jnp.where(x == 3, got[2], 0)
    mine = jnp.where((x == 1) & (core == 0), block, 0)
    second = mine + jnp.where(x == 2, got[0], 0) + jnp.where(x == 3, got[1], 0) + jnp.where(x == 0, got[2], 0)
    pair = jnp.stack([first, second])
    other = sibling(pair)
    low = jnp.where(core == 0, pair, other)
    high = jnp.where(core == 0, other, pair)
    return low[0], high[0], low[1]


def halves(v):
    high = v.astype(jnp.bfloat16)
    return high, (v - high.astype(jnp.float32)).astype(jnp.bfloat16)


def mm3(a, b):
    def dot(u, v):
        return jnp.dot(u, v, preferred_element_type=jnp.float32)

    return dot(a[0], b[0]) + (dot(a[0], b[1]) + dot(a[1], b[0]))


def picking_kernel(index_ref, tile_ref, near_ref, far_ref):
    v = tile_ref[...]
    high = v.astype(jnp.bfloat16)
    rest = v - high.astype(jnp.float32)
    middle = rest.astype(jnp.bfloat16)
    low = (rest - middle.astype(jnp.float32)).astype(jnp.bfloat16)
    rows = v.shape[0]
    half = near_ref.shape[0]
    for out_ref, start in ((far_ref, half), (near_ref, 0)):
        for at in range(0, half, 192):
            index = index_ref[start + at : start + at + 192, :]
            spots = lax.broadcasted_iota(jnp.int32, (192, rows), 1)
            chosen = (index == spots).astype(jnp.float32).astype(jnp.bfloat16)
            total = jnp.dot(chosen, low, preferred_element_type=jnp.float32)
            total = total + jnp.dot(chosen, middle, preferred_element_type=jnp.float32)
            total = total + jnp.dot(chosen, high, preferred_element_type=jnp.float32)
            out_ref[at : at + 192, :] = total


def pick_rows(index, tile):
    half = index.shape[0] // 2
    shape = jax.ShapeDtypeStruct((half, W), jnp.float32)
    return pl.pallas_call(
        picking_kernel,
        out_shape=(shape, shape),
        compiler_params=pltpu.CompilerParams(vmem_limit_bytes=32 << 20),
        cost_estimate=pl.CostEstimate(flops=2 * 1152 * 768 * 1152, bytes_accessed=3 << 20, transcendentals=0),
    )(index[:, None], tile)


def factor_kernel(facts_ref, *refs):
    pieces, nears = refs[:PROWS], refs[PROWS : 2 * PROWS]
    lower_ref, upper_ref, basis_ref, head_ref, corner, own = refs[2 * PROWS :]
    for i in range(PROWS):
        spot = pl.ds(pl.multiple_of(facts_ref[2 + i] * SUB, 16), SUB)
        for s in range(STEPS):
            own[s, spot, :] = nears[i][s * SUB : (s + 1) * SUB, :]
            for t in range(2):
                corner[2 * s + t, spot, :] = pieces[i][s, t]
    p, q = facts_ref[0], facts_ref[1]
    row = lax.broadcasted_iota(jnp.int32, (W, W), 0)
    col = lax.broadcasted_iota(jnp.int32, (W, W), 1)
    eye = (row == col).astype(jnp.float32)
    low = [halves(jnp.where(row > col, lower_ref[s], eye)) for s in range(STEPS)]
    up = [halves(jnp.where(row <= col, upper_ref[s], 0.0)) for s in range(STEPS)]
    z0 = own[0]
    u01 = halves(mm3(low[0], halves(corner[3])))
    u02 = halves(mm3(low[0], halves(corner[4])))
    u0 = mm3(low[0], halves(z0))
    u0h = halves(u0)
    l10 = mm3(halves(corner[0]), up[0])
    l10h = halves(l10)
    l20 = mm3(halves(corner[1]), up[0])
    l20h = halves(l20)
    u12 = halves(mm3(low[1], halves(corner[5] - mm3(l10h, u02))))
    l21 = mm3(halves(corner[2] - mm3(l20h, u01)), up[1])
    x1 = own[1] - mm3(l10h, u0h)
    u1 = mm3(low[1], halves(x1))
    x2 = own[2] - mm3(l20h, u0h) - mm3(halves(l21), halves(u1))
    u2 = mm3(low[2], halves(x2))

    @pl.when(p == 0)
    def _():
        head_ref[...] = jnp.where(q == 0, z0, u0)

    @pl.when(p == 1)
    def _():
        head_ref[...] = jnp.where(q == 0, l10, jnp.where(q == 1, x1, u1))

    @pl.when(p >= 2)
    def _():
        head_ref[...] = jnp.where(q == 0, l20, jnp.where(q == 1, l21, jnp.where(q == 2, x2, u2)))

    def basis(t, value):
        return jnp.where(q >= STEPS, value, jnp.where(q == t, -eye, 0.0))

    def keep(t, value):
        for j in range(PCOLS):
            at = (j * STEPS + t) * COLS
            basis_ref[at : at + COLS, :] = value[j * COLS : (j + 1) * COLS, :]

    g2 = mm3(up[2], halves(basis(2, u2)))
    keep(2, g2)
    g2 = halves(g2)
    g1 = mm3(up[1], halves(basis(1, u1) - mm3(u12, g2)))
    keep(1, g1)
    g0 = mm3(up[0], halves(basis(0, u0) - mm3(u01, halves(g1)) - mm3(u02, g2)))
    keep(0, g0)


def factors(p, q, held, ring, near, lower_inv, upper_inv):
    facts = jnp.stack([p, q] + held).astype(jnp.int32)
    vmem = pl.BlockSpec(memory_space=pltpu.VMEM)
    return pl.pallas_call(
        factor_kernel,
        out_shape=(
            jax.ShapeDtypeStruct((TOP, W), jnp.float32),
            jax.ShapeDtypeStruct((W, W), jnp.float32),
        ),
        in_specs=[pl.BlockSpec(memory_space=pltpu.SMEM)] + [vmem] * (2 * PROWS + 2),
        out_specs=(vmem, vmem),
        scratch_shapes=[
            pltpu.VMEM((2 * STEPS, W, W), jnp.float32),
            pltpu.VMEM((STEPS, W, W), jnp.float32),
        ],
        compiler_params=pltpu.CompilerParams(vmem_limit_bytes=44 << 20),
        cost_estimate=pl.CostEstimate(flops=40 * 3 * W**3, bytes_accessed=11 << 20, transcendentals=0),
    )(facts, *ring, *near, lower_inv, upper_inv)


def on_device(matrix, pivots, lower_inv, upper_inv):
    p = lax.axis_index("prow")
    q = lax.axis_index("pcol")
    x, core = p // 2, p % 2
    z, y = q // NY, q % NY
    tile = matrix[0, 0]
    rows = tile.shape[0]

    slots = jnp.arange(PROWS, dtype=jnp.int32)
    piece = ((x + slots % NX) % NX) * 2 + (core ^ (slots // NX))
    wanted = (
        piece[:, None, None] * SUB
        + (jnp.arange(STEPS, dtype=jnp.int32) * W)[None, :, None]
        + jnp.arange(SUB, dtype=jnp.int32)[None, None, :]
    ).reshape(-1)
    source = origin(wanted, pivots)
    block = source // W
    owned = block % PROWS == p
    local = jnp.where(owned, block // PROWS * W + source % W, -1)
    kept, sent = pick_rows(local, tile)
    summed = (kept + sibling(sent)).reshape(NX, STEPS * SUB, W)
    chunk = summed[0]
    for k in (1, 2, 3):
        chunk = chunk + x_shift(summed[k], k)

    parts = chunk.reshape(STEPS, SUB, W)
    twice = jnp.concatenate([parts, parts])
    off = lax.dynamic_slice_in_dim(twice, (y + 1) % STEPS, 2, axis=0)
    spread = jnp.where(z == 0, off, 0.0)
    for k in (1, 2, 3):
        spread = spread + from_z0(off, k)
    line = [spread] + [y_shift(spread, k) for k in (1, 2, 3)]
    line = placed(line, [(y - k) % NY for k in range(NY)], 0)[:STEPS]
    ring = [line] + [x_shift(line, k) for k in (1, 2, 3)]
    ring = ring + [sibling(v) for v in ring]
    held = [(x - k) % NX * 2 + (core ^ side) for side in (0, 1) for k in range(NX)]

    near = [chunk] + [x_shift(chunk, k) for k in (1, 2, 3)]
    near = near + [sibling(v) for v in near]
    basis, head = factors(p, q, held, ring, near, lower_inv, upper_inv)

    flat = tile.T
    part = jnp.where(z == 0, flat[: W // NZ], 0.0)
    for k in (1, 2, 3):
        part = part + from_z0(flat[k * (W // NZ) : (k + 1) * (W // NZ)], k)
    part = part.reshape(NY, COLS, rows)
    cut = [lax.dynamic_index_in_dim(part, (y + k) % NY, keepdims=False) for k in range(NY)]
    strips = cut[:1] + [y_shift(cut[k], k) for k in (1, 2, 3)]
    strips = placed(strips, [(y - k) % NY for k in range(NY)], 0)[:STEPS].reshape(STEPS * COLS, rows)
    tops = top_rows_everywhere(strips[:, :W], x, core)
    ids = jnp.arange(rows, dtype=jnp.int32)
    global_rows = (ids // W * PROWS + p) * W + ids % W
    came = origin(global_rows, pivots)
    is_bottom = global_rows >= TOP
    moved = is_bottom & (came < TOP)
    pick = jnp.where(moved, rows + came, ids)
    table = jnp.concatenate([strips, *tops], axis=1)
    chooser = (jnp.arange(rows + TOP, dtype=jnp.int32)[:, None] == pick[None, :]).astype(jnp.float32)
    strips = jnp.dot(table, chooser, precision=EXACT, preferred_element_type=jnp.float32)
    panel = lax.all_gather(strips, "pcol")
    panel = panel.reshape(TOP, rows)

    own_tops = jnp.concatenate(top_rows_everywhere(tile[:W], x, core))
    here = jnp.where(moved[:, None], own_tops[jnp.where(moved, came, 0)], tile)

    change = lax.dot_general(
        panel,
        basis,
        (((0,), (0,)), ((), ())),
        precision=HIGH,
        preferred_element_type=jnp.float32,
    )
    result = jnp.where(q >= STEPS, here, 0.0) - change
    first = jnp.where(p < STEPS, head, result[:W])
    return jnp.concatenate([first, result[W:]])[None, None]


def solution(mesh):
    return jax.shard_map(
        on_device,
        mesh=mesh,
        in_specs=(P("prow", "pcol", None, None), P(), P(), P()),
        out_specs=P("prow", "pcol", None, None),
        check_vma=False,
    )
```

```python
import jax
import jax.numpy as jnp
from jax import lax
from jax.experimental import pallas as pl
from jax.experimental.pallas import tpu as pltpu
from jax.sharding import PartitionSpec as P

W = 384
STEPS = 3
NX, NZ, NY = 4, 4, 4
PROWS, PCOLS = 8, 16
TOP = STEPS * W
SUB = W // PROWS
COLS = W // PCOLS
ROWS = 2 * W
F32 = jnp.float32
BF16 = jnp.bfloat16


def x_shift(v, k):
    return lax.ppermute(v, "prow", [(p, (p + 2 * k) % PROWS) for p in range(PROWS)])


def x_shift_top(v, k):
    return lax.ppermute(v, "prow", [(p, (p + 2 * k) % PROWS) for p in range(STEPS)])


def sibling(v):
    return lax.ppermute(v, "prow", [(p, p ^ 1) for p in range(PROWS)])


def to_odd(v):
    return lax.ppermute(v, "prow", [(p, p + 1) for p in range(0, PROWS, 2)])


def y_shift(v, k):
    return lax.ppermute(
        v, "pcol", [(z * NY + y, z * NY + (y + k) % NY) for z in range(NZ) for y in range(NY)]
    )


def from_z0(v, k):
    return lax.ppermute(v, "pcol", [(y, k * NY + y) for y in range(STEPS)])


def after(v, *others):
    return lax.optimization_barrier((v, *others))[0]


def placed(parts, places, axis):
    shape = parts[0].shape
    whole = jnp.zeros(shape[:axis] + (len(parts),) + shape[axis:], parts[0].dtype)
    for part, place in zip(parts, places):
        whole = lax.dynamic_update_slice_in_dim(whole, jnp.expand_dims(part, axis), place, axis=axis)
    return whole


def tops_by_x(block, got, x, core):
    first = jnp.where(x == 0, block, 0) + jnp.where(x == 1, got[0], 0)
    first = first + jnp.where(x == 2, got[1], 0) + jnp.where(x == 3, got[2], 0)
    even = core == 0
    second = jnp.where((x == 1) & even, block, 0) + jnp.where((x == 2) & even, got[0], 0)
    second = second + jnp.where((x == 3) & even, got[1], 0) + jnp.where((x == 0) & even, got[2], 0)
    return first, second


def halves(v):
    high = v.astype(BF16)
    return high, (v - high.astype(F32)).astype(BF16)


def thirds(v):
    high = v.astype(BF16).astype(F32)
    rest = v - high
    middle = rest.astype(BF16).astype(F32)
    return high, middle, rest - middle


def dot(u, v):
    return jnp.dot(u, v, preferred_element_type=F32)


def mm3(a, b):
    return dot(a[0], b[0]) + (dot(a[0], b[1]) + dot(a[1], b[0]))


def lhs3(v):
    high, low = v if isinstance(v, tuple) else halves(v)
    return jnp.concatenate([high, high, low], axis=1)


def rhs3(v):
    high, low = v if isinstance(v, tuple) else halves(v)
    return jnp.concatenate([high, low, high], axis=0)


def origin(v, pivots_ref, axis):
    for section in reversed(range(STEPS)):
        if axis == 1:
            listed = pivots_ref[section : section + 1, :].astype(F32)
        else:
            listed = pivots_ref[:, section : section + 1].astype(F32)
        shape = listed.shape
        here = (lax.broadcasted_iota(jnp.int32, shape, axis) + section * W).astype(F32)
        moves = jnp.where(v == listed, here - v, 0.0) + jnp.where(v == here, listed - v, 0.0)
        v = v + jnp.sum(moves, axis=axis, keepdims=True)
    return v


def third_of(n):
    return (n * 43) >> 7


def picking_kernel(facts_ref, pivots_ref, tile_ref, near_ref, far_ref, chosen_ref):
    p, x, core = facts_ref[0], facts_ref[1], facts_ref[2]
    size = STEPS * SUB
    row = lax.broadcasted_iota(jnp.int32, (size, 1), 0)
    late = (row >= SUB).astype(jnp.int32) + (row >= 2 * SUB).astype(jnp.int32)
    base = row + late * (W - SUB)
    for side in range(2):
        for k in range(NX):
            piece = ((x + k) % NX) * 2 + (core ^ side)
            source = origin((base + piece * SUB).astype(F32), pivots_ref, 1).astype(jnp.int32)
            block = third_of(source >> 7)
            local = source - block * W + (block >> 3) * W
            local = jnp.where((block & 7) == p, local, -1)
            spots = lax.broadcasted_iota(jnp.int32, (size, ROWS), 1)
            at = (side * NX + k) * size
            chosen_ref[at : at + size, :] = (local == spots).astype(F32).astype(BF16)
    high, middle, low = (part.astype(BF16) for part in thirds(tile_ref[...]))
    half = NX * size
    for out_ref, at in ((far_ref, half), (near_ref, 0)):
        chosen = chosen_ref[at : at + half, :]
        out_ref[...] = dot(chosen, low) + dot(chosen, middle) + dot(chosen, high)


def table_place(came, ids_global, core):
    swapped = jnp.where(came < W, came + W, came - W)
    place = jnp.where((core == 1) & (came < 2 * W), swapped, came)
    return jnp.where((ids_global >= TOP) & (came < TOP), place, -1)


def globals_of(ids, p):
    return ids + p * W + jnp.where(ids >= W, (PROWS - 1) * W, 0)


def strips_kernel(facts_ref, pivots_ref, strips_ref, a_ref, other_ref, b_ref, far_ref, out_ref):
    p, core = facts_ref[0], facts_ref[2]
    ids = globals_of(lax.broadcasted_iota(jnp.int32, (1, ROWS), 1), p)
    came = origin(ids.astype(F32), pivots_ref, 0).astype(jnp.int32)
    place = table_place(came, ids, core)
    spots = lax.broadcasted_iota(jnp.int32, (TOP, ROWS), 0)
    chosen = (spots == place).astype(F32).astype(BF16)
    last = jnp.where(core == 0, b_ref[...], far_ref[...])
    parts = thirds(jnp.concatenate([a_ref[...], other_ref[...], last], axis=1))
    size = parts[0].shape[0]
    stacked = jnp.concatenate(parts + (jnp.zeros((8, TOP), F32),), axis=0).astype(BF16)
    found = dot(stacked, chosen)
    found = found[2 * size : 3 * size] + found[size : 2 * size] + found[:size]
    out_ref[...] = jnp.where(place >= 0, found, strips_ref[...])


def rows_kernel(facts_ref, pivots_ref, tile_ref, tops_ref, out_ref, tops, sem):
    copy = pltpu.make_async_copy(tops_ref.at[:STEPS], tops, sem)
    copy.start()
    p = facts_ref[0]
    ids = globals_of(lax.broadcasted_iota(jnp.int32, (ROWS, 1), 0), p)
    came = origin(ids.astype(F32), pivots_ref, 1).astype(jnp.int32)
    place = table_place(came, ids, 0)
    spots = lax.broadcasted_iota(jnp.int32, (ROWS, TOP), 1)
    chosen = (spots == place).astype(F32).astype(BF16)
    copy.wait()
    high, middle, low = (part.astype(BF16) for part in thirds(tops[...].reshape(TOP, W)))
    found = dot(chosen, low) + dot(chosen, middle) + dot(chosen, high)
    out_ref[...] = jnp.where(place >= 0, found, tile_ref[...])


def triangles_kernel(lower_ref, upper_ref, low_ref, low2_ref, up_ref, up2_ref, tri, sems):
    row = lax.broadcasted_iota(jnp.int32, (W, W), 0)
    col = lax.broadcasted_iota(jnp.int32, (W, W), 1)
    for s in range(STEPS):
        tri[0, s], tri[1, s] = halves(jnp.where(row > col, lower_ref[s], (row == col).astype(F32)))
        tri[2, s], tri[3, s] = halves(jnp.where(row <= col, upper_ref[s], 0.0))
    copies = [
        pltpu.make_async_copy(tri.at[i], ref, sems.at[i])
        for i, ref in enumerate((low_ref, low2_ref, up_ref, up2_ref))
    ]
    for copy in copies:
        copy.start()
    for copy in copies:
        copy.wait()


def factor_kernel(facts_ref, *refs):
    pieces, nears = refs[:PROWS], refs[PROWS : 2 * PROWS]
    triangles = refs[2 * PROWS : 2 * PROWS + 4]
    basis_ref, head_ref, corner, own, tri, sems = refs[2 * PROWS + 4 :]
    copies = []
    for i in range(4):
        copies.append(pltpu.make_async_copy(triangles[i], tri.at[i], sems.at[2 * PROWS + i]))
    for i in range(PROWS):
        spot = pl.ds(pl.multiple_of(facts_ref[3 + i] * SUB, 16), SUB)
        copies.append(pltpu.make_async_copy(pieces[i], corner.at[:, :, spot, :], sems.at[2 * i]))
        copies.append(pltpu.make_async_copy(nears[i], own.at[:, spot, :], sems.at[2 * i + 1]))
    for copy in copies:
        copy.start()
    p, q = facts_ref[0], facts_ref[11]
    row = lax.broadcasted_iota(jnp.int32, (W, W), 0)
    col = lax.broadcasted_iota(jnp.int32, (W, W), 1)
    eye = (row == col).astype(F32)
    for copy in copies:
        copy.wait()
    low = [(tri[0, s], tri[1, s]) for s in range(STEPS)]
    up = [(tri[2, s], tri[3, s]) for s in range(STEPS)]
    z0 = own[0]
    wide = jnp.concatenate([corner[1, 1], corner[2, 0], z0], axis=1)
    wide = dot(lhs3(low[0]), rhs3(wide))
    wide3 = rhs3(wide)
    u01, u02, u0 = wide[:, :W], wide[:, W : 2 * W], wide[:, 2 * W :]
    tall = jnp.concatenate([corner[0, 0], corner[0, 1]], axis=0)
    tall = dot(lhs3(tall), rhs3(up[0]))
    l10, l20 = tall[:W], tall[W:]
    both = jnp.concatenate([corner[2, 1], own[1]], axis=1) - dot(lhs3(l10), wide3[:, W:])
    x1 = both[:, W:]
    both = dot(lhs3(low[1]), rhs3(both))
    u12, u1 = both[:, :W], both[:, W:]
    l20_3 = lhs3(l20)
    l21 = dot(lhs3(corner[1, 0] - dot(l20_3, wide3[:, :W])), rhs3(up[1]))
    x2 = own[2] - dot(l20_3, wide3[:, 2 * W :]) - dot(lhs3(l21), rhs3(u1))
    u2 = dot(lhs3(low[2]), rhs3(x2))

    @pl.when(p == 0)
    def _():
        head_ref[...] = jnp.where(q == 0, z0, u0)

    @pl.when(p == 1)
    def _():
        head_ref[...] = jnp.where(q == 0, l10, jnp.where(q == 1, x1, u1))

    @pl.when(p >= 2)
    def _():
        head_ref[...] = jnp.where(q == 0, l20, jnp.where(q == 1, l21, jnp.where(q == 2, x2, u2)))

    def basis(t, value):
        return jnp.where(q >= STEPS, value, jnp.where(q == t, -eye, 0.0))

    def keep(t, value):
        for j in range(PCOLS):
            at = (j * STEPS + t) * COLS
            basis_ref[at : at + COLS, :] = value[j * COLS : (j + 1) * COLS, :]

    g2 = dot(lhs3(up[2]), rhs3(basis(2, u2)))
    keep(2, g2)
    g2_3 = rhs3(g2)
    g1 = dot(lhs3(up[1]), rhs3(basis(1, u1) - dot(lhs3(u12), g2_3)))
    keep(1, g1)
    left = jnp.concatenate([lhs3(u01), lhs3(u02)], axis=1)
    right = jnp.concatenate([rhs3(g1), g2_3], axis=0)
    g0 = dot(lhs3(up[0]), rhs3(basis(0, u0) - dot(left, right)))
    keep(0, g0)


def final_kernel(facts_ref, panel_ref, basis_ref, here_ref, head_ref, out_ref, panel, sems):
    p, q = facts_ref[0], facts_ref[11]
    copies = [
        pltpu.make_async_copy(panel_ref.at[:, i * W : (i + 1) * W], panel.at[i], sems.at[i])
        for i in range(2)
    ]
    for copy in copies:
        copy.start()
    g = halves(basis_ref[...])

    def rows(i):
        span = slice(i * W, (i + 1) * W)
        a = halves(panel[i].T)
        out_ref[span, :] = jnp.where(q >= STEPS, here_ref[span, :], 0.0) - mm3(a, g)

    copies[0].wait()

    @pl.when(p < STEPS)
    def _():
        out_ref[:W, :] = head_ref[...]

    @pl.when(p >= STEPS)
    def _():
        rows(0)

    copies[1].wait()
    rows(1)


SMEM = pl.BlockSpec(memory_space=pltpu.SMEM)
WHOLE = pl.BlockSpec()
HBM = pl.BlockSpec(memory_space=pltpu.HBM)


def cost(flops, moved):
    return pl.CostEstimate(flops=flops, bytes_accessed=moved, transcendentals=0)


def shape(*sizes):
    return jax.ShapeDtypeStruct(sizes, F32)


def params(mib):
    return pltpu.CompilerParams(vmem_limit_bytes=mib << 20)


def on_device(matrix, pivots, lower_inv, upper_inv):
    p = lax.axis_index("prow")
    q = lax.axis_index("pcol")
    x, core = p // 2, p % 2
    z, y = q // NY, q % NY
    tile = matrix[0, 0]
    held = [(x - k) % NX * 2 + (core ^ side) for side in (0, 1) for k in range(NX)]
    facts = jnp.stack([p, x, core] + held + [q]).astype(jnp.int32)

    flat = tile.T
    got = [from_z0(flat[k * (W // NZ) : (k + 1) * (W // NZ)], k) for k in (1, 2, 3)]

    own_tops = lax.all_gather(tile[:W], "prow")

    kept, sent = pl.pallas_call(
        picking_kernel,
        out_shape=(shape(ROWS // 4 * 3, W),) * 2,
        in_specs=[SMEM, WHOLE, WHOLE],
        scratch_shapes=[pltpu.VMEM((TOP, ROWS), BF16)],
        compiler_params=params(14),
        cost_estimate=cost(2 * TOP * ROWS * TOP, 3 << 20),
    )(facts, pivots, tile)

    *got, kept, sent = lax.optimization_barrier((*got, kept, sent))
    crossed = sibling(sent)
    part = jnp.where(z == 0, flat[: W // NZ], 0.0)
    for v in got:
        part = part + v
    part = part.reshape(NY, COLS, ROWS)
    cut = [lax.dynamic_index_in_dim(part, (y + k) % NY, keepdims=False) for k in range(NY)]
    got = [y_shift(cut[k], k) for k in (1, 2, 3)]

    triangles = pl.pallas_call(
        triangles_kernel,
        out_shape=(jax.ShapeDtypeStruct((STEPS, W, W), BF16),) * 4,
        in_specs=[WHOLE] * 2,
        out_specs=(HBM,) * 4,
        scratch_shapes=[pltpu.VMEM((4, STEPS, W, W), BF16), pltpu.SemaphoreType.DMA((4,))],
        compiler_params=params(16),
        cost_estimate=cost(1 << 23, 7 << 20),
    )(lower_inv, upper_inv)

    *got, crossed, t1, t2, t3, t4 = lax.optimization_barrier((*got, crossed, *triangles))
    triangles = (t1, t2, t3, t4)
    summed = (kept + crossed).reshape(NX, STEPS * SUB, W)
    strips = placed(cut[:1] + got, [(y - k) % NY for k in range(NY)], 0)[:STEPS]
    strips = strips.reshape(STEPS * COLS, ROWS)
    strip_tops = strips[:, :W]
    tops_got = [x_shift_top(strip_tops, k) for k in (1, 2, 3)]

    around = [x_shift(summed[k], k) for k in (1, 2, 3)]

    *tops_got, summed = lax.optimization_barrier((*tops_got, summed))
    a, b = tops_by_x(strip_tops, tops_got, x, core)
    a_other, b_far = sibling(a), to_odd(b)

    *around, a_other, b_far = lax.optimization_barrier((*around, a_other, b_far))
    strips = pl.pallas_call(
        strips_kernel,
        out_shape=shape(STEPS * COLS, ROWS),
        in_specs=[SMEM] + [WHOLE] * 6,
        compiler_params=params(14),
        cost_estimate=cost(2 * 216 * TOP * ROWS, 1 << 20),
    )(facts, pivots.T, strips, a, a_other, b, b_far)
    panel = lax.all_gather(strips, "pcol").reshape(TOP, ROWS)
    chunk = summed[0]
    for v in around:
        chunk = chunk + v
    parts = chunk.reshape(STEPS, SUB, W)
    twice = jnp.concatenate([parts, parts])
    off = lax.dynamic_slice_in_dim(twice, (y + 1) % STEPS, 2, axis=0)
    got = [from_z0(off, k) for k in (1, 2, 3)]
    near = [parts] + [x_shift(parts, k) for k in (1, 2, 3)]

    got_near = lax.optimization_barrier((*got, strips, *near))
    got, strips, near = got_near[:3], got_near[3], list(got_near[4:])
    near = near + [sibling(v) for v in near]
    spread = jnp.where(z == 0, off, 0.0)
    for v in got:
        spread = spread + v
    line = [spread] + [y_shift(spread, k) for k in (1, 2, 3)]
    line = placed(line, [(y - k) % NY for k in range(NY)], 0)[:STEPS]
    ring = [line] + [x_shift(line, k) for k in (1, 2, 3)]

    here = pl.pallas_call(
        rows_kernel,
        out_shape=shape(ROWS, W),
        in_specs=[SMEM, WHOLE, WHOLE, HBM],
        scratch_shapes=[pltpu.VMEM((STEPS, W, W), F32), pltpu.SemaphoreType.DMA],
        compiler_params=params(60),
        cost_estimate=cost(2 * ROWS * TOP * TOP, 5 << 20),
    )(facts, pivots, tile, own_tops)

    *ring, here = lax.optimization_barrier((*ring, here))
    ring = ring + [sibling(v) for v in ring]

    basis, head = pl.pallas_call(
        factor_kernel,
        out_shape=(shape(TOP, W), shape(W, W)),
        in_specs=[SMEM] + [HBM] * (2 * PROWS + 4),
        scratch_shapes=[
            pltpu.VMEM((STEPS, 2, W, W), F32),
            pltpu.VMEM((STEPS, W, W), F32),
            pltpu.VMEM((4, STEPS, W, W), BF16),
            pltpu.SemaphoreType.DMA((2 * PROWS + 4,)),
        ],
        compiler_params=params(60),
        cost_estimate=cost(40 * 3 * W**3, 11 << 20),
    )(facts, *ring, *near, *triangles)

    result = pl.pallas_call(
        final_kernel,
        out_shape=shape(ROWS, W),
        in_specs=[SMEM, HBM] + [WHOLE] * 3,
        scratch_shapes=[pltpu.VMEM((2, TOP, W), F32), pltpu.SemaphoreType.DMA((2,))],
        compiler_params=params(60),
        cost_estimate=cost(6 * ROWS * TOP * W, 8 << 20),
    )(facts, panel, basis, here, head)
    return result[None, None]


def solution(mesh):
    return jax.shard_map(
        on_device,
        mesh=mesh,
        in_specs=(P("prow", "pcol", None, None), P(), P(), P()),
        out_specs=P("prow", "pcol", None, None),
        check_vma=False,
    )
```

```python
import jax
import jax.numpy as jnp
from jax import lax
from jax.experimental import pallas as pl
from jax.experimental.pallas import tpu as pltpu
from jax.sharding import PartitionSpec as P

W = 384
STEPS = 3
NX, NZ, NY = 4, 4, 4
PROWS, PCOLS = 8, 16
TOP = STEPS * W
SUB = W // PROWS
COLS = W // PCOLS
ROWS = 2 * W
F32 = jnp.float32
BF16 = jnp.bfloat16


def x_shift(v, k):
    return lax.ppermute(v, "prow", [(p, (p + 2 * k) % PROWS) for p in range(PROWS)])


def sibling(v):
    return lax.ppermute(v, "prow", [(p, p ^ 1) for p in range(PROWS)])


def y_shift(v, k):
    return lax.ppermute(
        v, "pcol", [(z * NY + y, z * NY + (y + k) % NY) for z in range(NZ) for y in range(NY)]
    )


def from_z0(v, k):
    return lax.ppermute(v, "pcol", [(y, k * NY + y) for y in range(STEPS)])


def after(v, *others):
    return lax.optimization_barrier((v, *others))[0]


def placed(parts, places, axis):
    shape = parts[0].shape
    whole = jnp.zeros(shape[:axis] + (len(parts),) + shape[axis:], parts[0].dtype)
    for part, place in zip(parts, places):
        whole = lax.dynamic_update_slice_in_dim(whole, jnp.expand_dims(part, axis), place, axis=axis)
    return whole


def tops_by_x(block, got, x, core):
    first = jnp.where(x == 0, block, 0) + jnp.where(x == 1, got[0], 0)
    first = first + jnp.where(x == 2, got[1], 0) + jnp.where(x == 3, got[2], 0)
    even = core == 0
    second = jnp.where((x == 1) & even, block, 0) + jnp.where((x == 2) & even, got[0], 0)
    second = second + jnp.where((x == 3) & even, got[1], 0) + jnp.where((x == 0) & even, got[2], 0)
    return first, second


def halves(v):
    high = v.astype(BF16)
    return high, (v - high.astype(F32)).astype(BF16)


def thirds(v):
    high = v.astype(BF16).astype(F32)
    rest = v - high
    middle = rest.astype(BF16).astype(F32)
    return high, middle, rest - middle


def dot(u, v):
    return jnp.dot(u, v, preferred_element_type=F32)


def mm3(a, b):
    return dot(a[0], b[0]) + (dot(a[0], b[1]) + dot(a[1], b[0]))


def lhs3(v):
    high, low = v if isinstance(v, tuple) else halves(v)
    return jnp.concatenate([high, high, low], axis=1)


def rhs3(v):
    high, low = v if isinstance(v, tuple) else halves(v)
    return jnp.concatenate([high, low, high], axis=0)


def origin(v, pivots_ref, axis):
    for section in reversed(range(STEPS)):
        if axis == 1:
            listed = pivots_ref[section : section + 1, :].astype(F32)
        else:
            listed = pivots_ref[:, section : section + 1].astype(F32)
        shape = listed.shape
        here = (lax.broadcasted_iota(jnp.int32, shape, axis) + section * W).astype(F32)
        moves = jnp.where(v == listed, here - v, 0.0) + jnp.where(v == here, listed - v, 0.0)
        v = v + jnp.sum(moves, axis=axis, keepdims=True)
    return v


def third_of(n):
    return (n * 43) >> 7


def picking_kernel(facts_ref, pivots_ref, tile_ref, near_ref, far_ref, chosen_ref):
    p, x, core = facts_ref[0], facts_ref[1], facts_ref[2]
    size = STEPS * SUB
    row = lax.broadcasted_iota(jnp.int32, (size, 1), 0)
    late = (row >= SUB).astype(jnp.int32) + (row >= 2 * SUB).astype(jnp.int32)
    base = row + late * (W - SUB)
    for side in range(2):
        for k in range(NX):
            piece = ((x + k) % NX) * 2 + (core ^ side)
            source = origin((base + piece * SUB).astype(F32), pivots_ref, 1).astype(jnp.int32)
            block = third_of(source >> 7)
            local = source - block * W + (block >> 3) * W
            local = jnp.where((block & 7) == p, local, -1)
            spots = lax.broadcasted_iota(jnp.int32, (size, ROWS), 1)
            at = (side * NX + k) * size
            chosen_ref[at : at + size, :] = (local == spots).astype(F32).astype(BF16)
    high, middle, low = (part.astype(BF16) for part in thirds(tile_ref[...]))
    half = NX * size
    for out_ref, at in ((far_ref, half), (near_ref, 0)):
        chosen = chosen_ref[at : at + half, :]
        out_ref[...] = dot(chosen, low) + dot(chosen, middle) + dot(chosen, high)


def table_place(came, ids_global, core):
    swapped = jnp.where(came < W, came + W, came - W)
    place = jnp.where((core == 1) & (came < 2 * W), swapped, came)
    return jnp.where((ids_global >= TOP) & (came < TOP), place, -1)


def globals_of(ids, p):
    return ids + p * W + jnp.where(ids >= W, (PROWS - 1) * W, 0)


def strips_kernel(facts_ref, pivots_ref, strips_ref, a_ref, other_ref, b_ref, far_ref, out_ref):
    p, core = facts_ref[0], facts_ref[2]
    ids = globals_of(lax.broadcasted_iota(jnp.int32, (1, ROWS), 1), p)
    came = origin(ids.astype(F32), pivots_ref, 0).astype(jnp.int32)
    place = table_place(came, ids, core)
    spots = lax.broadcasted_iota(jnp.int32, (TOP, ROWS), 0)
    chosen = (spots == place).astype(F32).astype(BF16)
    last = jnp.where(core == 0, b_ref[...], far_ref[...])
    parts = thirds(jnp.concatenate([a_ref[...], other_ref[...], last], axis=1))
    size = parts[0].shape[0]
    stacked = jnp.concatenate(parts + (jnp.zeros((8, TOP), F32),), axis=0).astype(BF16)
    found = dot(stacked, chosen)
    found = found[2 * size : 3 * size] + found[size : 2 * size] + found[:size]
    out_ref[...] = jnp.where(place >= 0, found, strips_ref[...])


def rows_kernel(facts_ref, pivots_ref, tile_ref, tops_ref, out_ref, tops, sem):
    copy = pltpu.make_async_copy(tops_ref.at[:STEPS], tops, sem)
    copy.start()
    p = facts_ref[0]
    ids = globals_of(lax.broadcasted_iota(jnp.int32, (ROWS, 1), 0), p)
    came = origin(ids.astype(F32), pivots_ref, 1).astype(jnp.int32)
    place = table_place(came, ids, 0)
    spots = lax.broadcasted_iota(jnp.int32, (ROWS, TOP), 1)
    chosen = (spots == place).astype(F32).astype(BF16)
    copy.wait()
    high, middle, low = (part.astype(BF16) for part in thirds(tops[...].reshape(TOP, W)))
    found = dot(chosen, low) + dot(chosen, middle) + dot(chosen, high)
    out_ref[...] = jnp.where(place >= 0, found, tile_ref[...])


def triangles_kernel(lower_ref, upper_ref, low_ref, low2_ref, up_ref, up2_ref, tri, sems):
    row = lax.broadcasted_iota(jnp.int32, (W, W), 0)
    col = lax.broadcasted_iota(jnp.int32, (W, W), 1)
    for s in range(STEPS):
        tri[0, s], tri[1, s] = halves(jnp.where(row > col, lower_ref[s], (row == col).astype(F32)))
        tri[2, s], tri[3, s] = halves(jnp.where(row <= col, upper_ref[s], 0.0))
    copies = [
        pltpu.make_async_copy(tri.at[i], ref, sems.at[i])
        for i, ref in enumerate((low_ref, low2_ref, up_ref, up2_ref))
    ]
    for copy in copies:
        copy.start()
    for copy in copies:
        copy.wait()


def factor_kernel(facts_ref, *refs):
    pieces, nears = refs[:PROWS], refs[PROWS : 2 * PROWS]
    triangles = refs[2 * PROWS : 2 * PROWS + 4]
    basis_ref, head_ref, corner, own, tri, sems = refs[2 * PROWS + 4 :]
    copies = []
    for i in range(4):
        copies.append(pltpu.make_async_copy(triangles[i], tri.at[i], sems.at[2 * PROWS + i]))
    for i in range(PROWS):
        spot = pl.ds(pl.multiple_of(facts_ref[3 + i] * SUB, 16), SUB)
        copies.append(pltpu.make_async_copy(pieces[i], corner.at[:, :, spot, :], sems.at[2 * i]))
        copies.append(pltpu.make_async_copy(nears[i], own.at[:, spot, :], sems.at[2 * i + 1]))
    for copy in copies:
        copy.start()
    p, q = facts_ref[0], facts_ref[11]
    row = lax.broadcasted_iota(jnp.int32, (W, W), 0)
    col = lax.broadcasted_iota(jnp.int32, (W, W), 1)
    eye = (row == col).astype(F32)
    for copy in copies:
        copy.wait()
    low = [(tri[0, s], tri[1, s]) for s in range(STEPS)]
    up = [(tri[2, s], tri[3, s]) for s in range(STEPS)]
    z0 = own[0]
    wide = jnp.concatenate([corner[1, 1], corner[2, 0], z0], axis=1)
    wide = dot(lhs3(low[0]), rhs3(wide))
    wide3 = rhs3(wide)
    u01, u02, u0 = wide[:, :W], wide[:, W : 2 * W], wide[:, 2 * W :]
    tall = jnp.concatenate([corner[0, 0], corner[0, 1]], axis=0)
    tall = dot(lhs3(tall), rhs3(up[0]))
    l10, l20 = tall[:W], tall[W:]
    both = jnp.concatenate([corner[2, 1], own[1]], axis=1) - dot(lhs3(l10), wide3[:, W:])
    x1 = both[:, W:]
    both = dot(lhs3(low[1]), rhs3(both))
    u12, u1 = both[:, :W], both[:, W:]
    l20_3 = lhs3(l20)
    l21 = dot(lhs3(corner[1, 0] - dot(l20_3, wide3[:, :W])), rhs3(up[1]))
    x2 = own[2] - dot(l20_3, wide3[:, 2 * W :]) - dot(lhs3(l21), rhs3(u1))
    u2 = dot(lhs3(low[2]), rhs3(x2))

    @pl.when(p == 0)
    def _():
        head_ref[...] = jnp.where(q == 0, z0, u0)

    @pl.when(p == 1)
    def _():
        head_ref[...] = jnp.where(q == 0, l10, jnp.where(q == 1, x1, u1))

    @pl.when(p >= 2)
    def _():
        head_ref[...] = jnp.where(q == 0, l20, jnp.where(q == 1, l21, jnp.where(q == 2, x2, u2)))

    def basis(t, value):
        return jnp.where(q >= STEPS, value, jnp.where(q == t, -eye, 0.0))

    def keep(t, value):
        for j in range(PCOLS):
            at = (j * STEPS + t) * COLS
            basis_ref[at : at + COLS, :] = value[j * COLS : (j + 1) * COLS, :]

    g2 = dot(lhs3(up[2]), rhs3(basis(2, u2)))
    keep(2, g2)
    g2_3 = rhs3(g2)
    g1 = dot(lhs3(up[1]), rhs3(basis(1, u1) - dot(lhs3(u12), g2_3)))
    keep(1, g1)
    left = jnp.concatenate([lhs3(u01), lhs3(u02)], axis=1)
    right = jnp.concatenate([rhs3(g1), g2_3], axis=0)
    g0 = dot(lhs3(up[0]), rhs3(basis(0, u0) - dot(left, right)))
    keep(0, g0)


def final_kernel(facts_ref, panel_ref, basis_ref, here_ref, head_ref, out_ref, panel, sems):
    p, q = facts_ref[0], facts_ref[11]
    copies = [
        pltpu.make_async_copy(panel_ref.at[:, i * W : (i + 1) * W], panel.at[i], sems.at[i])
        for i in range(2)
    ]
    for copy in copies:
        copy.start()
    g = halves(basis_ref[...])

    def rows(i):
        span = slice(i * W, (i + 1) * W)
        a = halves(panel[i].T)
        out_ref[span, :] = jnp.where(q >= STEPS, here_ref[span, :], 0.0) - mm3(a, g)

    copies[0].wait()

    @pl.when(p < STEPS)
    def _():
        out_ref[:W, :] = head_ref[...]

    @pl.when(p >= STEPS)
    def _():
        rows(0)

    copies[1].wait()
    rows(1)


SMEM = pl.BlockSpec(memory_space=pltpu.SMEM)
WHOLE = pl.BlockSpec()
HBM = pl.BlockSpec(memory_space=pltpu.HBM)


def cost(flops, moved):
    return pl.CostEstimate(flops=flops, bytes_accessed=moved, transcendentals=0)


def shape(*sizes):
    return jax.ShapeDtypeStruct(sizes, F32)


def params(mib):
    return pltpu.CompilerParams(vmem_limit_bytes=mib << 20)


def on_device(matrix, pivots, lower_inv, upper_inv):
    p = lax.axis_index("prow")
    q = lax.axis_index("pcol")
    x, core = p // 2, p % 2
    z, y = q // NY, q % NY
    tile = matrix[0, 0]
    held = [(x - k) % NX * 2 + (core ^ side) for side in (0, 1) for k in range(NX)]
    facts = jnp.stack([p, x, core] + held + [q]).astype(jnp.int32)

    flat = tile.T
    got = [from_z0(flat[k * (W // NZ) : (k + 1) * (W // NZ)], k) for k in (1, 2, 3)]

    own_tops = lax.all_gather(tile[:W], "prow")

    kept, sent = pl.pallas_call(
        picking_kernel,
        out_shape=(shape(ROWS // 4 * 3, W),) * 2,
        in_specs=[SMEM, WHOLE, WHOLE],
        scratch_shapes=[pltpu.VMEM((TOP, ROWS), BF16)],
        compiler_params=params(14),
        cost_estimate=cost(2 * TOP * ROWS * TOP, 3 << 20),
    )(facts, pivots, tile)

    *got, kept, sent = lax.optimization_barrier((*got, kept, sent))
    crossed = sibling(sent)
    part = jnp.where(z == 0, flat[: W // NZ], 0.0)
    for v in got:
        part = part + v
    part = part.reshape(NY, COLS, ROWS)
    cut = [lax.dynamic_index_in_dim(part, (y + k) % NY, keepdims=False) for k in range(NY)]
    got = [y_shift(cut[k], k) for k in (1, 2, 3)]

    triangles = pl.pallas_call(
        triangles_kernel,
        out_shape=(jax.ShapeDtypeStruct((STEPS, W, W), BF16),) * 4,
        in_specs=[WHOLE] * 2,
        out_specs=(HBM,) * 4,
        scratch_shapes=[pltpu.VMEM((4, STEPS, W, W), BF16), pltpu.SemaphoreType.DMA((4,))],
        compiler_params=params(16),
        cost_estimate=cost(1 << 23, 7 << 20),
    )(lower_inv, upper_inv)

    *got, crossed, t1, t2, t3, t4 = lax.optimization_barrier((*got, crossed, *triangles))
    triangles = (t1, t2, t3, t4)
    summed = (kept + crossed).reshape(NX, STEPS * SUB, W)
    strips = placed(cut[:1] + got, [(y - k) % NY for k in range(NY)], 0)[:STEPS]
    strips = strips.reshape(STEPS * COLS, ROWS)
    strip_tops = strips[:, :W]
    tops_got = [x_shift(strip_tops, k) for k in (1, 2, 3)]

    around = [x_shift(summed[k], k) for k in (1, 2, 3)]

    *tops_got, summed = lax.optimization_barrier((*tops_got, summed))
    a, b = tops_by_x(strip_tops, tops_got, x, core)
    a_other, b_far = sibling(a), sibling(b)

    *around, a_other, b_far = lax.optimization_barrier((*around, a_other, b_far))
    strips = pl.pallas_call(
        strips_kernel,
        out_shape=shape(STEPS * COLS, ROWS),
        in_specs=[SMEM] + [WHOLE] * 6,
        compiler_params=params(14),
        cost_estimate=cost(2 * 216 * TOP * ROWS, 1 << 20),
    )(facts, pivots.T, strips, a, a_other, b, b_far)
    panel = lax.all_gather(strips, "pcol").reshape(TOP, ROWS)
    chunk = summed[0]
    for v in around:
        chunk = chunk + v
    parts = chunk.reshape(STEPS, SUB, W)
    twice = jnp.concatenate([parts, parts])
    off = lax.dynamic_slice_in_dim(twice, (y + 1) % STEPS, 2, axis=0)
    got = [from_z0(off, k) for k in (1, 2, 3)]

    *got, strips, early = lax.optimization_barrier((*got, strips, parts))
    spread = jnp.where(z == 0, off, 0.0)
    for v in got:
        spread = spread + v
    line = [spread] + [y_shift(spread, k) for k in (1, 2, 3)]
    near = [early] + [x_shift(early, k) for k in (1, 2, 3)]
    line_near = lax.optimization_barrier((*line, *near))
    line, near = line_near[:NY], list(line_near[NY:])
    near = near + [sibling(v) for v in near]
    line = placed(line, [(y - k) % NY for k in range(NY)], 0)[:STEPS]
    ring = [line] + [x_shift(line, k) for k in (1, 2, 3)]

    here = pl.pallas_call(
        rows_kernel,
        out_shape=shape(ROWS, W),
        in_specs=[SMEM, WHOLE, WHOLE, HBM],
        scratch_shapes=[pltpu.VMEM((STEPS, W, W), F32), pltpu.SemaphoreType.DMA],
        compiler_params=params(60),
        cost_estimate=cost(2 * ROWS * TOP * TOP, 5 << 20),
    )(facts, pivots, tile, own_tops)

    *ring, here = lax.optimization_barrier((*ring, here))
    ring = ring + [sibling(v) for v in ring]

    basis, head = pl.pallas_call(
        factor_kernel,
        out_shape=(shape(TOP, W), shape(W, W)),
        in_specs=[SMEM] + [HBM] * (2 * PROWS + 4),
        scratch_shapes=[
            pltpu.VMEM((STEPS, 2, W, W), F32),
            pltpu.VMEM((STEPS, W, W), F32),
            pltpu.VMEM((4, STEPS, W, W), BF16),
            pltpu.SemaphoreType.DMA((2 * PROWS + 4,)),
        ],
        compiler_params=params(60),
        cost_estimate=cost(40 * 3 * W**3, 11 << 20),
    )(facts, *ring, *near, *triangles)

    result = pl.pallas_call(
        final_kernel,
        out_shape=shape(ROWS, W),
        in_specs=[SMEM, HBM] + [WHOLE] * 3,
        scratch_shapes=[pltpu.VMEM((2, TOP, W), F32), pltpu.SemaphoreType.DMA((2,))],
        compiler_params=params(60),
        cost_estimate=cost(6 * ROWS * TOP * W, 8 << 20),
    )(facts, panel, basis, here, head)
    return result[None, None]


def solution(mesh):
    return jax.shard_map(
        on_device,
        mesh=mesh,
        in_specs=(P("prow", "pcol", None, None), P(), P(), P()),
        out_specs=P("prow", "pcol", None, None),
        check_vma=False,
    )
```

```python
import jax
import jax.numpy as jnp
from jax import lax
from jax.experimental import pallas as pl
from jax.experimental.pallas import tpu as pltpu
from jax.sharding import PartitionSpec as P

W = 384
STEPS = 3
NX, NZ, NY = 4, 4, 4
PROWS, PCOLS = 8, 16
TOP = STEPS * W
SUB = W // PROWS
COLS = W // PCOLS
ROWS = 2 * W
F32 = jnp.float32
BF16 = jnp.bfloat16


def x_shift(v, k):
    return lax.ppermute(v, "prow", [(p, (p + 2 * k) % PROWS) for p in range(PROWS)])


def sibling(v):
    return lax.ppermute(v, "prow", [(p, p ^ 1) for p in range(PROWS)])


def y_shift(v, k):
    return lax.ppermute(
        v, "pcol", [(z * NY + y, z * NY + (y + k) % NY) for z in range(NZ) for y in range(NY)]
    )


def from_z0(v, k):
    return lax.ppermute(v, "pcol", [(y, k * NY + y) for y in range(STEPS)])


def after(v, *others):
    return lax.optimization_barrier((v, *others))[0]


def placed(parts, places, axis):
    shape = parts[0].shape
    whole = jnp.zeros(shape[:axis] + (len(parts),) + shape[axis:], parts[0].dtype)
    for part, place in zip(parts, places):
        whole = lax.dynamic_update_slice_in_dim(whole, jnp.expand_dims(part, axis), place, axis=axis)
    return whole


def tops_by_x(block, got, x, core):
    first = jnp.where(x == 0, block, 0) + jnp.where(x == 1, got[0], 0)
    first = first + jnp.where(x == 2, got[1], 0) + jnp.where(x == 3, got[2], 0)
    even = core == 0
    second = jnp.where((x == 1) & even, block, 0) + jnp.where((x == 2) & even, got[0], 0)
    second = second + jnp.where((x == 3) & even, got[1], 0) + jnp.where((x == 0) & even, got[2], 0)
    return first, second


def halves(v):
    high = v.astype(BF16)
    return high, (v - high.astype(F32)).astype(BF16)


def thirds(v):
    high = v.astype(BF16).astype(F32)
    rest = v - high
    middle = rest.astype(BF16).astype(F32)
    return high, middle, rest - middle


def dot(u, v):
    return jnp.dot(u, v, preferred_element_type=F32)


def mm3(a, b):
    return dot(a[0], b[0]) + (dot(a[0], b[1]) + dot(a[1], b[0]))


def lhs3(v):
    high, low = v if isinstance(v, tuple) else halves(v)
    return jnp.concatenate([high, high, low], axis=1)


def rhs3(v):
    high, low = v if isinstance(v, tuple) else halves(v)
    return jnp.concatenate([high, low, high], axis=0)


def origin(v, pivots_ref, axis):
    for section in reversed(range(STEPS)):
        if axis == 1:
            listed = pivots_ref[section : section + 1, :].astype(F32)
        else:
            listed = pivots_ref[:, section : section + 1].astype(F32)
        shape = listed.shape
        here = (lax.broadcasted_iota(jnp.int32, shape, axis) + section * W).astype(F32)
        moves = jnp.where(v == listed, here - v, 0.0) + jnp.where(v == here, listed - v, 0.0)
        v = v + jnp.sum(moves, axis=axis, keepdims=True)
    return v


def third_of(n):
    return (n * 43) >> 7


def picking_kernel(facts_ref, pivots_ref, tile_ref, near_ref, far_ref, chosen_ref):
    p, x, core = facts_ref[0], facts_ref[1], facts_ref[2]
    size = STEPS * SUB
    row = lax.broadcasted_iota(jnp.int32, (size, 1), 0)
    late = (row >= SUB).astype(jnp.int32) + (row >= 2 * SUB).astype(jnp.int32)
    base = row + late * (W - SUB)
    for side in range(2):
        for k in range(NX):
            piece = ((x + k) % NX) * 2 + (core ^ side)
            source = origin((base + piece * SUB).astype(F32), pivots_ref, 1).astype(jnp.int32)
            block = third_of(source >> 7)
            local = source - block * W + (block >> 3) * W
            local = jnp.where((block & 7) == p, local, -1)
            spots = lax.broadcasted_iota(jnp.int32, (size, ROWS), 1)
            at = (side * NX + k) * size
            chosen_ref[at : at + size, :] = (local == spots).astype(F32).astype(BF16)
    high, middle, low = (part.astype(BF16) for part in thirds(tile_ref[...]))
    half = NX * size
    for out_ref, at in ((far_ref, half), (near_ref, 0)):
        chosen = chosen_ref[at : at + half, :]
        out_ref[...] = dot(chosen, low) + dot(chosen, middle) + dot(chosen, high)


def table_place(came, ids_global, core):
    swapped = jnp.where(came < W, came + W, came - W)
    place = jnp.where((core == 1) & (came < 2 * W), swapped, came)
    return jnp.where((ids_global >= TOP) & (came < TOP), place, -1)


def globals_of(ids, p):
    return ids + p * W + jnp.where(ids >= W, (PROWS - 1) * W, 0)


def strips_kernel(facts_ref, pivots_ref, strips_ref, a_ref, other_ref, b_ref, far_ref, out_ref):
    p, core = facts_ref[0], facts_ref[2]
    ids = globals_of(lax.broadcasted_iota(jnp.int32, (1, ROWS), 1), p)
    came = origin(ids.astype(F32), pivots_ref, 0).astype(jnp.int32)
    place = table_place(came, ids, core)
    spots = lax.broadcasted_iota(jnp.int32, (TOP, ROWS), 0)
    chosen = (spots == place).astype(F32).astype(BF16)
    last = jnp.where(core == 0, b_ref[...], far_ref[...])
    parts = thirds(jnp.concatenate([a_ref[...], other_ref[...], last], axis=1))
    size = parts[0].shape[0]
    stacked = jnp.concatenate(parts + (jnp.zeros((8, TOP), F32),), axis=0).astype(BF16)
    found = dot(stacked, chosen)
    found = found[2 * size : 3 * size] + found[size : 2 * size] + found[:size]
    out_ref[...] = jnp.where(place >= 0, found, strips_ref[...])


def rows_kernel(facts_ref, pivots_ref, tile_ref, tops_ref, out_ref, tops, sem):
    copy = pltpu.make_async_copy(tops_ref.at[:STEPS], tops, sem)
    copy.start()
    p = facts_ref[0]
    ids = globals_of(lax.broadcasted_iota(jnp.int32, (ROWS, 1), 0), p)
    came = origin(ids.astype(F32), pivots_ref, 1).astype(jnp.int32)
    place = table_place(came, ids, 0)
    spots = lax.broadcasted_iota(jnp.int32, (ROWS, TOP), 1)
    chosen = (spots == place).astype(F32).astype(BF16)
    copy.wait()
    high, middle, low = (part.astype(BF16) for part in thirds(tops[...].reshape(TOP, W)))
    found = dot(chosen, low) + dot(chosen, middle) + dot(chosen, high)
    out_ref[...] = jnp.where(place >= 0, found, tile_ref[...])


def triangles_kernel(lower_ref, upper_ref, low_ref, low2_ref, up_ref, up2_ref, tri, sems):
    row = lax.broadcasted_iota(jnp.int32, (W, W), 0)
    col = lax.broadcasted_iota(jnp.int32, (W, W), 1)
    for s in range(STEPS):
        tri[0, s], tri[1, s] = halves(jnp.where(row > col, lower_ref[s], (row == col).astype(F32)))
        tri[2, s], tri[3, s] = halves(jnp.where(row <= col, upper_ref[s], 0.0))
    copies = [
        pltpu.make_async_copy(tri.at[i], ref, sems.at[i])
        for i, ref in enumerate((low_ref, low2_ref, up_ref, up2_ref))
    ]
    for copy in copies:
        copy.start()
    for copy in copies:
        copy.wait()


def factor_kernel(facts_ref, *refs):
    pieces, nears = refs[:PROWS], refs[PROWS : 2 * PROWS]
    triangles = refs[2 * PROWS : 2 * PROWS + 4]
    basis_ref, head_ref, corner, own, tri, sems = refs[2 * PROWS + 4 :]
    pairs = [(triangles[i], tri.at[i]) for i in range(4)]
    for source, kept in ((nears, own), (pieces, corner)):
        for i in range(PROWS):
            spot = pl.ds(pl.multiple_of(facts_ref[3 + i] * SUB, 16), SUB)
            pairs.append((source[i], kept.at[:, spot, :] if kept is own else kept.at[:, :, spot, :]))
    copies = [pltpu.make_async_copy(*pair, sems.at[i]) for i, pair in enumerate(pairs)]
    for copy in copies:
        copy.start()
    for copy in copies[: 4 + PROWS]:
        copy.wait()
    low = [(tri[0, s], tri[1, s]) for s in range(STEPS)]
    up = [(tri[2, s], tri[3, s]) for s in range(STEPS)]
    z0 = own[0]
    low0 = lhs3(low[0])
    u0 = dot(low0, rhs3(z0))
    u0_3 = rhs3(u0)
    for copy in copies[4 + PROWS :]:
        copy.wait()
    p, q = facts_ref[0], facts_ref[11]
    row = lax.broadcasted_iota(jnp.int32, (W, W), 0)
    col = lax.broadcasted_iota(jnp.int32, (W, W), 1)
    eye = (row == col).astype(F32)
    wide = dot(low0, rhs3(jnp.concatenate([corner[1, 1], corner[2, 0]], axis=1)))
    u01, u02 = wide[:, :W], wide[:, W:]
    wide3 = jnp.concatenate([rhs3(u02), u0_3], axis=1)
    tall = dot(lhs3(jnp.concatenate([corner[0, 0], corner[0, 1]], axis=0)), rhs3(up[0]))
    l10, l20 = tall[:W], tall[W:]
    both = jnp.concatenate([corner[2, 1], own[1]], axis=1) - dot(lhs3(l10), wide3)
    x1 = both[:, W:]
    both = dot(lhs3(low[1]), rhs3(both))
    u12, u1 = both[:, :W], both[:, W:]
    l20_3 = lhs3(l20)
    l21 = dot(lhs3(corner[1, 0] - dot(l20_3, rhs3(u01))), rhs3(up[1]))
    x2 = own[2] - dot(l20_3, u0_3) - dot(lhs3(l21), rhs3(u1))
    u2 = dot(lhs3(low[2]), rhs3(x2))
    head = jnp.where(q == 0, l20, jnp.where(q == 1, l21, jnp.where(q == 2, x2, u2)))
    head = jnp.where(p == 1, jnp.where(q == 0, l10, jnp.where(q == 1, x1, u1)), head)
    head_ref[...] = jnp.where(p == 0, jnp.where(q == 0, z0, u0), head)

    def basis(t, value):
        return jnp.where(q >= STEPS, value, jnp.where(q == t, -eye, 0.0))

    def keep(t, value):
        for j in range(PCOLS):
            at = (j * STEPS + t) * COLS
            basis_ref[at : at + COLS, :] = value[j * COLS : (j + 1) * COLS, :]

    g2 = dot(lhs3(up[2]), rhs3(basis(2, u2)))
    keep(2, g2)
    g2_3 = rhs3(g2)
    g1 = dot(lhs3(up[1]), rhs3(basis(1, u1) - dot(lhs3(u12), g2_3)))
    keep(1, g1)
    left = jnp.concatenate([lhs3(u01), lhs3(u02)], axis=1)
    right = jnp.concatenate([rhs3(g1), g2_3], axis=0)
    g0 = dot(lhs3(up[0]), rhs3(basis(0, u0) - dot(left, right)))
    keep(0, g0)


def final_kernel(facts_ref, panel_ref, basis_ref, here_ref, head_ref, out_ref, panel, sems):
    p, q = facts_ref[0], facts_ref[11]
    copies = [
        pltpu.make_async_copy(panel_ref.at[:, i * W : (i + 1) * W], panel.at[i], sems.at[i])
        for i in range(2)
    ]
    for copy in copies:
        copy.start()
    g = halves(basis_ref[...])

    def rows(i):
        span = slice(i * W, (i + 1) * W)
        a = halves(panel[i].T)
        out_ref[span, :] = jnp.where(q >= STEPS, here_ref[span, :], 0.0) - mm3(a, g)

    copies[0].wait()

    @pl.when(p < STEPS)
    def _():
        out_ref[:W, :] = head_ref[...]

    @pl.when(p >= STEPS)
    def _():
        rows(0)

    copies[1].wait()
    rows(1)


SMEM = pl.BlockSpec(memory_space=pltpu.SMEM)
WHOLE = pl.BlockSpec()
HBM = pl.BlockSpec(memory_space=pltpu.HBM)


def cost(flops, moved):
    return pl.CostEstimate(flops=flops, bytes_accessed=moved, transcendentals=0)


def shape(*sizes):
    return jax.ShapeDtypeStruct(sizes, F32)


def params(mib):
    return pltpu.CompilerParams(vmem_limit_bytes=mib << 20)


def on_device(matrix, pivots, lower_inv, upper_inv):
    p = lax.axis_index("prow")
    q = lax.axis_index("pcol")
    x, core = p // 2, p % 2
    z, y = q // NY, q % NY
    tile = matrix[0, 0]
    held = [(x - k) % NX * 2 + (core ^ side) for side in (0, 1) for k in range(NX)]
    facts = jnp.stack([p, x, core] + held + [q]).astype(jnp.int32)

    flat = tile.T
    got = [from_z0(flat[k * (W // NZ) : (k + 1) * (W // NZ)], k) for k in (1, 2, 3)]

    own_tops = lax.all_gather(tile[:W], "prow")

    kept, sent = pl.pallas_call(
        picking_kernel,
        out_shape=(shape(ROWS // 4 * 3, W),) * 2,
        in_specs=[SMEM, WHOLE, WHOLE],
        scratch_shapes=[pltpu.VMEM((TOP, ROWS), BF16)],
        compiler_params=params(14),
        cost_estimate=cost(2 * TOP * ROWS * TOP, 3 << 20),
    )(facts, pivots, tile)

    *got, kept, sent = lax.optimization_barrier((*got, kept, sent))
    crossed = sibling(sent)
    part = jnp.where(z == 0, flat[: W // NZ], 0.0)
    for v in got:
        part = part + v
    part = part.reshape(NY, COLS, ROWS)
    cut = [lax.dynamic_index_in_dim(part, (y + k) % NY, keepdims=False) for k in range(NY)]
    got = [y_shift(cut[k], k) for k in (1, 2, 3)]

    triangles = pl.pallas_call(
        triangles_kernel,
        out_shape=(jax.ShapeDtypeStruct((STEPS, W, W), BF16),) * 4,
        in_specs=[WHOLE] * 2,
        out_specs=(HBM,) * 4,
        scratch_shapes=[pltpu.VMEM((4, STEPS, W, W), BF16), pltpu.SemaphoreType.DMA((4,))],
        compiler_params=params(16),
        cost_estimate=cost(1 << 23, 7 << 20),
    )(lower_inv, upper_inv)

    *got, crossed, t1, t2, t3, t4 = lax.optimization_barrier((*got, crossed, *triangles))
    triangles = (t1, t2, t3, t4)
    summed = (kept + crossed).reshape(NX, STEPS * SUB, W)
    strips = placed(cut[:1] + got, [(y - k) % NY for k in range(NY)], 0)[:STEPS]
    strips = strips.reshape(STEPS * COLS, ROWS)
    strip_tops = strips[:, :W]
    tops_got = [x_shift(strip_tops, k) for k in (1, 2, 3)]

    around = [x_shift(summed[k], k) for k in (1, 2, 3)]

    *tops_got, summed = lax.optimization_barrier((*tops_got, summed))
    a, b = tops_by_x(strip_tops, tops_got, x, core)
    a_other, b_far = sibling(a), sibling(b)

    *around, a_other, b_far = lax.optimization_barrier((*around, a_other, b_far))
    strips = pl.pallas_call(
        strips_kernel,
        out_shape=shape(STEPS * COLS, ROWS),
        in_specs=[SMEM] + [WHOLE] * 6,
        compiler_params=params(14),
        cost_estimate=cost(2 * 216 * TOP * ROWS, 1 << 20),
    )(facts, pivots.T, strips, a, a_other, b, b_far)
    panel = lax.all_gather(strips, "pcol").reshape(TOP, ROWS)
    chunk = summed[0]
    for v in around:
        chunk = chunk + v
    parts = chunk.reshape(STEPS, SUB, W)
    twice = jnp.concatenate([parts, parts])
    off = lax.dynamic_slice_in_dim(twice, (y + 1) % STEPS, 2, axis=0)
    got = [from_z0(off, k) for k in (1, 2, 3)]

    *got, strips, early = lax.optimization_barrier((*got, strips, parts))
    spread = jnp.where(z == 0, off, 0.0)
    for v in got:
        spread = spread + v
    line = [spread] + [y_shift(spread, k) for k in (1, 2, 3)]
    near = [early] + [x_shift(early, k) for k in (1, 2, 3)]
    line_near = lax.optimization_barrier((*line, *near))
    line, near = line_near[:NY], list(line_near[NY:])
    near = near + [sibling(v) for v in near]
    line = placed(line, [(y - k) % NY for k in range(NY)], 0)[:STEPS]
    ring = [line] + [x_shift(line, k) for k in (1, 2, 3)]

    here = pl.pallas_call(
        rows_kernel,
        out_shape=shape(ROWS, W),
        in_specs=[SMEM, WHOLE, WHOLE, HBM],
        scratch_shapes=[pltpu.VMEM((STEPS, W, W), F32), pltpu.SemaphoreType.DMA],
        compiler_params=params(60),
        cost_estimate=cost(2 * ROWS * TOP * TOP, 5 << 20),
    )(facts, pivots, tile, own_tops)

    *ring, here = lax.optimization_barrier((*ring, here))
    ring = ring + [sibling(v) for v in ring]

    basis, head = pl.pallas_call(
        factor_kernel,
        out_shape=(shape(TOP, W), shape(W, W)),
        in_specs=[SMEM] + [HBM] * (2 * PROWS + 4),
        scratch_shapes=[
            pltpu.VMEM((STEPS, 2, W, W), F32),
            pltpu.VMEM((STEPS, W, W), F32),
            pltpu.VMEM((4, STEPS, W, W), BF16),
            pltpu.SemaphoreType.DMA((2 * PROWS + 4,)),
        ],
        compiler_params=params(60),
        cost_estimate=cost(40 * 3 * W**3, 11 << 20),
    )(facts, *ring, *near, *triangles)

    result = pl.pallas_call(
        final_kernel,
        out_shape=shape(ROWS, W),
        in_specs=[SMEM, HBM] + [WHOLE] * 3,
        scratch_shapes=[pltpu.VMEM((2, TOP, W), F32), pltpu.SemaphoreType.DMA((2,))],
        compiler_params=params(60),
        cost_estimate=cost(6 * ROWS * TOP * W, 8 << 20),
    )(facts, panel, basis, here, head)
    return result[None, None]


def solution(mesh):
    return jax.shard_map(
        on_device,
        mesh=mesh,
        in_specs=(P("prow", "pcol", None, None), P(), P(), P()),
        out_specs=P("prow", "pcol", None, None),
        check_vma=False,
    )
```

```python
import jax
import jax.numpy as jnp
from jax import lax
from jax.experimental import pallas as pl
from jax.experimental.pallas import tpu as pltpu
from jax.sharding import PartitionSpec as P

W = 384
STEPS = 3
NX, NZ, NY = 4, 4, 4
PROWS, PCOLS = 8, 16
TOP = STEPS * W
SUB = W // PROWS
COLS = W // PCOLS
ROWS = 2 * W
F32 = jnp.float32
BF16 = jnp.bfloat16


def x_shift(v, k):
    return lax.ppermute(v, "prow", [(p, (p + 2 * k) % PROWS) for p in range(PROWS)])


def sibling(v):
    return lax.ppermute(v, "prow", [(p, p ^ 1) for p in range(PROWS)])


def y_shift(v, k):
    return lax.ppermute(
        v, "pcol", [(z * NY + y, z * NY + (y + k) % NY) for z in range(NZ) for y in range(NY)]
    )


def from_z0(v, k):
    return lax.ppermute(v, "pcol", [(y, k * NY + y) for y in range(STEPS)])


def after(v, *others):
    return lax.optimization_barrier((v, *others))[0]


def placed(parts, places, axis):
    shape = parts[0].shape
    whole = jnp.zeros(shape[:axis] + (len(parts),) + shape[axis:], parts[0].dtype)
    for part, place in zip(parts, places):
        whole = lax.dynamic_update_slice_in_dim(whole, jnp.expand_dims(part, axis), place, axis=axis)
    return whole


def tops_by_x(block, got, x, core):
    first = jnp.where(x == 0, block, 0) + jnp.where(x == 1, got[0], 0)
    first = first + jnp.where(x == 2, got[1], 0) + jnp.where(x == 3, got[2], 0)
    even = core == 0
    second = jnp.where((x == 1) & even, block, 0) + jnp.where((x == 2) & even, got[0], 0)
    second = second + jnp.where((x == 3) & even, got[1], 0) + jnp.where((x == 0) & even, got[2], 0)
    return first, second


def halves(v):
    high = v.astype(BF16)
    return high, (v - high.astype(F32)).astype(BF16)


def thirds(v):
    high = v.astype(BF16).astype(F32)
    rest = v - high
    middle = rest.astype(BF16).astype(F32)
    return high, middle, rest - middle


def dot(u, v):
    return jnp.dot(u, v, preferred_element_type=F32)


def mm3(a, b):
    return dot(a[0], b[0]) + (dot(a[0], b[1]) + dot(a[1], b[0]))


def lhs3(v):
    high, low = v if isinstance(v, tuple) else halves(v)
    return jnp.concatenate([high, high, low], axis=1)


def rhs3(v):
    high, low = v if isinstance(v, tuple) else halves(v)
    return jnp.concatenate([high, low, high], axis=0)


def origin(v, pivots_ref, axis):
    for section in reversed(range(STEPS)):
        if axis == 1:
            listed = pivots_ref[section : section + 1, :].astype(F32)
        else:
            listed = pivots_ref[:, section : section + 1].astype(F32)
        shape = listed.shape
        here = (lax.broadcasted_iota(jnp.int32, shape, axis) + section * W).astype(F32)
        moves = jnp.where(v == listed, here - v, 0.0) + jnp.where(v == here, listed - v, 0.0)
        v = v + jnp.sum(moves, axis=axis, keepdims=True)
    return v


def third_of(n):
    return (n * 43) >> 7


def picking_kernel(facts_ref, pivots_ref, tile_ref, near_ref, far_ref, chosen_ref):
    p, x, core = facts_ref[0], facts_ref[1], facts_ref[2]
    size = STEPS * SUB
    row = lax.broadcasted_iota(jnp.int32, (size, 1), 0)
    late = (row >= SUB).astype(jnp.int32) + (row >= 2 * SUB).astype(jnp.int32)
    base = row + late * (W - SUB)
    for side in range(2):
        for k in range(NX):
            piece = ((x + k) % NX) * 2 + (core ^ side)
            source = origin((base + piece * SUB).astype(F32), pivots_ref, 1).astype(jnp.int32)
            block = third_of(source >> 7)
            local = source - block * W + (block >> 3) * W
            local = jnp.where((block & 7) == p, local, -1)
            spots = lax.broadcasted_iota(jnp.int32, (size, ROWS), 1)
            at = (side * NX + k) * size
            chosen_ref[at : at + size, :] = (local == spots).astype(F32).astype(BF16)
    high, middle, low = (part.astype(BF16) for part in thirds(tile_ref[...]))
    half = NX * size
    for out_ref, at in ((far_ref, half), (near_ref, 0)):
        chosen = chosen_ref[at : at + half, :]
        out_ref[...] = dot(chosen, low) + dot(chosen, middle) + dot(chosen, high)


def table_place(came, ids_global, core):
    swapped = jnp.where(came < W, came + W, came - W)
    place = jnp.where((core == 1) & (came < 2 * W), swapped, came)
    return jnp.where((ids_global >= TOP) & (came < TOP), place, -1)


def globals_of(ids, p):
    return ids + p * W + jnp.where(ids >= W, (PROWS - 1) * W, 0)


def strips_kernel(facts_ref, pivots_ref, strips_ref, a_ref, other_ref, b_ref, far_ref, out_ref):
    p, core = facts_ref[0], facts_ref[2]
    ids = globals_of(lax.broadcasted_iota(jnp.int32, (1, ROWS), 1), p)
    came = origin(ids.astype(F32), pivots_ref, 0).astype(jnp.int32)
    place = table_place(came, ids, core)
    spots = lax.broadcasted_iota(jnp.int32, (TOP, ROWS), 0)
    chosen = (spots == place).astype(F32).astype(BF16)
    last = jnp.where(core == 0, b_ref[...], far_ref[...])
    parts = thirds(jnp.concatenate([a_ref[...], other_ref[...], last], axis=1))
    size = parts[0].shape[0]
    stacked = jnp.concatenate(parts + (jnp.zeros((8, TOP), F32),), axis=0).astype(BF16)
    found = dot(stacked, chosen)
    found = found[2 * size : 3 * size] + found[size : 2 * size] + found[:size]
    out_ref[...] = jnp.where(place >= 0, found, strips_ref[...])


def rows_kernel(facts_ref, pivots_ref, tile_ref, tops_ref, out_ref, tops, sem):
    copy = pltpu.make_async_copy(tops_ref.at[:STEPS], tops, sem)
    copy.start()
    p = facts_ref[0]
    ids = globals_of(lax.broadcasted_iota(jnp.int32, (ROWS, 1), 0), p)
    came = origin(ids.astype(F32), pivots_ref, 1).astype(jnp.int32)
    place = table_place(came, ids, 0)
    spots = lax.broadcasted_iota(jnp.int32, (ROWS, TOP), 1)
    chosen = (spots == place).astype(F32).astype(BF16)
    copy.wait()
    high, middle, low = (part.astype(BF16) for part in thirds(tops[...].reshape(TOP, W)))
    found = dot(chosen, low) + dot(chosen, middle) + dot(chosen, high)
    out_ref[...] = jnp.where(place >= 0, found, tile_ref[...])


def triangles_kernel(lower_ref, upper_ref, low_ref, low2_ref, up_ref, up2_ref, tri, sems):
    row = lax.broadcasted_iota(jnp.int32, (W, W), 0)
    col = lax.broadcasted_iota(jnp.int32, (W, W), 1)
    for s in range(STEPS):
        tri[0, s], tri[1, s] = halves(jnp.where(row > col, lower_ref[s], (row == col).astype(F32)))
        tri[2, s], tri[3, s] = halves(jnp.where(row <= col, upper_ref[s], 0.0))
    copies = [
        pltpu.make_async_copy(tri.at[i], ref, sems.at[i])
        for i, ref in enumerate((low_ref, low2_ref, up_ref, up2_ref))
    ]
    for copy in copies:
        copy.start()
    for copy in copies:
        copy.wait()


def factor_kernel(facts_ref, *refs):
    pieces, nears = refs[:PROWS], refs[PROWS : 2 * PROWS]
    triangles = refs[2 * PROWS : 2 * PROWS + 4]
    basis_ref, head_ref, corner, own, tri, sems = refs[2 * PROWS + 4 :]
    pairs = [(triangles[i], tri.at[i]) for i in range(4)]
    for source, kept in ((nears, own), (pieces, corner)):
        for i in range(PROWS):
            spot = pl.ds(pl.multiple_of(facts_ref[3 + i] * SUB, 16), SUB)
            pairs.append((source[i], kept.at[:, spot, :] if kept is own else kept.at[:, :, spot, :]))
    copies = [pltpu.make_async_copy(*pair, sems.at[i]) for i, pair in enumerate(pairs)]
    for copy in copies:
        copy.start()
    for copy in copies[: 4 + PROWS]:
        copy.wait()
    low = [(tri[0, s], tri[1, s]) for s in range(STEPS)]
    up = [(tri[2, s], tri[3, s]) for s in range(STEPS)]
    z0 = own[0]
    low0 = lhs3(low[0])
    u0 = dot(low0, rhs3(z0))
    u0_3 = rhs3(u0)
    for copy in copies[4 + PROWS :]:
        copy.wait()
    p, q = facts_ref[0], facts_ref[11]
    row = lax.broadcasted_iota(jnp.int32, (W, W), 0)
    col = lax.broadcasted_iota(jnp.int32, (W, W), 1)
    eye = (row == col).astype(F32)
    wide = dot(low0, rhs3(jnp.concatenate([corner[1, 1], corner[2, 0]], axis=1)))
    u01, u02 = wide[:, :W], wide[:, W:]
    wide3 = jnp.concatenate([rhs3(u02), u0_3], axis=1)
    tall = dot(lhs3(jnp.concatenate([corner[0, 0], corner[0, 1]], axis=0)), rhs3(up[0]))
    l10, l20 = tall[:W], tall[W:]
    both = jnp.concatenate([corner[2, 1], own[1]], axis=1) - dot(lhs3(l10), wide3)
    x1 = both[:, W:]
    both = dot(lhs3(low[1]), rhs3(both))
    u12, u1 = both[:, :W], both[:, W:]
    l20_3 = lhs3(l20)
    l21 = dot(lhs3(corner[1, 0] - dot(l20_3, rhs3(u01))), rhs3(up[1]))
    x2 = own[2] - dot(l20_3, u0_3) - dot(lhs3(l21), rhs3(u1))
    u2 = dot(lhs3(low[2]), rhs3(x2))
    head = jnp.where(q == 0, l20, jnp.where(q == 1, l21, jnp.where(q == 2, x2, u2)))
    head = jnp.where(p == 1, jnp.where(q == 0, l10, jnp.where(q == 1, x1, u1)), head)
    head_ref[...] = jnp.where(p == 0, jnp.where(q == 0, z0, u0), head)

    def basis(t, value):
        return jnp.where(q >= STEPS, value, jnp.where(q == t, -eye, 0.0))

    def keep(t, value):
        for j in range(PCOLS):
            at = (j * STEPS + t) * COLS
            basis_ref[at : at + COLS, :] = value[j * COLS : (j + 1) * COLS, :]

    g2 = dot(lhs3(up[2]), rhs3(basis(2, u2)))
    keep(2, g2)
    g2_3 = rhs3(g2)
    g1 = dot(lhs3(up[1]), rhs3(basis(1, u1) - dot(lhs3(u12), g2_3)))
    keep(1, g1)
    left = jnp.concatenate([lhs3(u01), lhs3(u02)], axis=1)
    right = jnp.concatenate([rhs3(g1), g2_3], axis=0)
    g0 = dot(lhs3(up[0]), rhs3(basis(0, u0) - dot(left, right)))
    keep(0, g0)


def final_kernel(facts_ref, panel_hbm, basis_hbm, here_hbm, head_hbm, out_ref, panel, basis_ref, here_ref, head_ref, sems):
    p, q = facts_ref[0], facts_ref[11]
    pairs = [(panel_hbm.at[:, i * W : (i + 1) * W], panel.at[i]) for i in range(2)]
    pairs = [(basis_hbm, basis_ref), pairs[0], pairs[1], (here_hbm, here_ref), (head_hbm, head_ref)]
    copies = [pltpu.make_async_copy(*pair, sems.at[i]) for i, pair in enumerate(pairs)]
    for copy in copies:
        copy.start()
    copies[0].wait()
    g = halves(basis_ref[...])

    def rows(i):
        span = slice(i * W, (i + 1) * W)
        a = halves(panel[i].T)
        out_ref[span, :] = jnp.where(q >= STEPS, here_ref[span, :], 0.0) - mm3(a, g)

    for copy in (copies[1], copies[3], copies[4]):
        copy.wait()

    @pl.when(p < STEPS)
    def _():
        out_ref[:W, :] = head_ref[...]

    @pl.when(p >= STEPS)
    def _():
        rows(0)

    copies[2].wait()
    rows(1)


SMEM = pl.BlockSpec(memory_space=pltpu.SMEM)
WHOLE = pl.BlockSpec()
HBM = pl.BlockSpec(memory_space=pltpu.HBM)


def cost(flops, moved):
    return pl.CostEstimate(flops=flops, bytes_accessed=moved, transcendentals=0)


def shape(*sizes):
    return jax.ShapeDtypeStruct(sizes, F32)


def params(mib):
    return pltpu.CompilerParams(vmem_limit_bytes=mib << 20)


def on_device(matrix, pivots, lower_inv, upper_inv):
    p = lax.axis_index("prow")
    q = lax.axis_index("pcol")
    x, core = p // 2, p % 2
    z, y = q // NY, q % NY
    tile = matrix[0, 0]
    held = [(x - k) % NX * 2 + (core ^ side) for side in (0, 1) for k in range(NX)]
    facts = jnp.stack([p, x, core] + held + [q]).astype(jnp.int32)

    flat = tile.T
    got = [from_z0(flat[k * (W // NZ) : (k + 1) * (W // NZ)], k) for k in (1, 2, 3)]

    own_tops = lax.all_gather(tile[:W], "prow")

    kept, sent = pl.pallas_call(
        picking_kernel,
        out_shape=(shape(ROWS // 4 * 3, W),) * 2,
        in_specs=[SMEM, WHOLE, WHOLE],
        scratch_shapes=[pltpu.VMEM((TOP, ROWS), BF16)],
        compiler_params=params(14),
        cost_estimate=cost(2 * TOP * ROWS * TOP, 3 << 20),
    )(facts, pivots, tile)

    *got, kept, sent = lax.optimization_barrier((*got, kept, sent))
    crossed = sibling(sent)
    part = jnp.where(z == 0, flat[: W // NZ], 0.0)
    for v in got:
        part = part + v
    part = part.reshape(NY, COLS, ROWS)
    cut = [lax.dynamic_index_in_dim(part, (y + k) % NY, keepdims=False) for k in range(NY)]
    got = [y_shift(cut[k], k) for k in (1, 2, 3)]

    triangles = pl.pallas_call(
        triangles_kernel,
        out_shape=(jax.ShapeDtypeStruct((STEPS, W, W), BF16),) * 4,
        in_specs=[WHOLE] * 2,
        out_specs=(HBM,) * 4,
        scratch_shapes=[pltpu.VMEM((4, STEPS, W, W), BF16), pltpu.SemaphoreType.DMA((4,))],
        compiler_params=params(16),
        cost_estimate=cost(1 << 23, 7 << 20),
    )(lower_inv, upper_inv)

    *got, crossed, t1, t2, t3, t4 = lax.optimization_barrier((*got, crossed, *triangles))
    triangles = (t1, t2, t3, t4)
    summed = (kept + crossed).reshape(NX, STEPS * SUB, W)
    strips = placed(cut[:1] + got, [(y - k) % NY for k in range(NY)], 0)[:STEPS]
    strips = strips.reshape(STEPS * COLS, ROWS)
    strip_tops = strips[:, :W]
    tops_got = [x_shift(strip_tops, k) for k in (1, 2, 3)]

    around = [x_shift(summed[k], k) for k in (1, 2, 3)]

    *tops_got, summed = lax.optimization_barrier((*tops_got, summed))
    a, b = tops_by_x(strip_tops, tops_got, x, core)
    a_other, b_far = sibling(a), sibling(b)

    *around, a_other, b_far = lax.optimization_barrier((*around, a_other, b_far))
    strips = pl.pallas_call(
        strips_kernel,
        out_shape=shape(STEPS * COLS, ROWS),
        in_specs=[SMEM] + [WHOLE] * 6,
        compiler_params=params(14),
        cost_estimate=cost(2 * 216 * TOP * ROWS, 1 << 20),
    )(facts, pivots.T, strips, a, a_other, b, b_far)
    panel = lax.all_gather(strips, "pcol").reshape(TOP, ROWS)
    chunk = summed[0]
    for v in around:
        chunk = chunk + v
    parts = chunk.reshape(STEPS, SUB, W)
    twice = jnp.concatenate([parts, parts])
    off = lax.dynamic_slice_in_dim(twice, (y + 1) % STEPS, 2, axis=0)
    got = [from_z0(off, k) for k in (1, 2, 3)]

    *got, strips, early = lax.optimization_barrier((*got, strips, parts))
    spread = jnp.where(z == 0, off, 0.0)
    for v in got:
        spread = spread + v
    line = [spread] + [y_shift(spread, k) for k in (1, 2, 3)]
    near = [early] + [x_shift(early, k) for k in (1, 2, 3)]
    line_near = lax.optimization_barrier((*line, *near))
    line, near = line_near[:NY], list(line_near[NY:])
    near = near + [sibling(v) for v in near]
    line = placed(line, [(y - k) % NY for k in range(NY)], 0)[:STEPS]
    ring = [line] + [x_shift(line, k) for k in (1, 2, 3)]

    here = pl.pallas_call(
        rows_kernel,
        out_shape=shape(ROWS, W),
        in_specs=[SMEM, WHOLE, WHOLE, HBM],
        scratch_shapes=[pltpu.VMEM((STEPS, W, W), F32), pltpu.SemaphoreType.DMA],
        compiler_params=params(60),
        cost_estimate=cost(2 * ROWS * TOP * TOP, 5 << 20),
    )(facts, pivots, tile, own_tops)

    *ring, here = lax.optimization_barrier((*ring, here))
    ring = ring + [sibling(v) for v in ring]

    basis, head = pl.pallas_call(
        factor_kernel,
        out_shape=(shape(TOP, W), shape(W, W)),
        in_specs=[SMEM] + [HBM] * (2 * PROWS + 4),
        scratch_shapes=[
            pltpu.VMEM((STEPS, 2, W, W), F32),
            pltpu.VMEM((STEPS, W, W), F32),
            pltpu.VMEM((4, STEPS, W, W), BF16),
            pltpu.SemaphoreType.DMA((2 * PROWS + 4,)),
        ],
        compiler_params=params(60),
        cost_estimate=cost(40 * 3 * W**3, 11 << 20),
    )(facts, *ring, *near, *triangles)

    result = pl.pallas_call(
        final_kernel,
        out_shape=shape(ROWS, W),
        in_specs=[SMEM] + [HBM] * 4,
        scratch_shapes=[
            pltpu.VMEM((2, TOP, W), F32),
            pltpu.VMEM((TOP, W), F32),
            pltpu.VMEM((ROWS, W), F32),
            pltpu.VMEM((W, W), F32),
            pltpu.SemaphoreType.DMA((5,)),
        ],
        compiler_params=params(60),
        cost_estimate=cost(6 * ROWS * TOP * W, 8 << 20),
    )(facts, panel, basis, here, head)
    return result[None, None]


def solution(mesh):
    return jax.shard_map(
        on_device,
        mesh=mesh,
        in_specs=(P("prow", "pcol", None, None), P(), P(), P()),
        out_specs=P("prow", "pcol", None, None),
        check_vma=False,
    )
```
